128 devices in a mesh: row: 8 (over x, z_hi), col: 8 (over z_lo, y), mat: 2 (over core).
Axes of the slice: x: 4, y: 4, z: 4 (z_hi: 2, z_lo: 2; z = z_hi * 2 + z_lo), core: 2. Of those that a mesh axis runs over, the one named last changes fastest.
Arguments:
- gradient: bfloat16 [2, 5120, 5120], P('mat', 'row', 'col'), may hold values from -6 to 6
- left_basis: bfloat16 [2, 5120, 5120], P('mat', 'col', 'row'), may hold values from -0.078125 to 0.078125
- right_basis: bfloat16 [2, 5120, 5120], P('mat', 'col', 'row'), may hold values from -0.078125 to 0.078125
- first_moment: float32 [2, 5120, 5120], P('mat', 'row', 'col'), may hold values from -6 to 6
- second_moment: float32 [2, 5120, 5120], P('mat', 'row', 'col'), may hold values from 0.1 to 10
Outputs:
- update: bfloat16 [2, 5120, 5120], P('mat', 'row', 'col')
- new_first: float32 [2, 5120, 5120], P('mat', 'row', 'col')
- new_second: float32 [2, 5120, 5120], P('mat', 'row', 'col')
The draws below stay inside these ranges and needn't reach their ends.
All inputs are finite; a program needn't handle non-finite values.
Results may differ from the reference program's by a relative error of at most 0.02.
Values may be sent and summed in bfloat16 or wider, within the bound.
No kernel may reach another device: no remote copies, remote signals or barrier semaphores. Data moves between devices by JAX's collectives and lax.ppermute only.
A program may use at most 128 MiB of HBM per device.

```python
import math
import jax
import jax.numpy as jnp
from jax import lax

D = 5120
MATS = 2
N_ROW = 8
N_COL = 8


def shard_levels(stream_key, shape, shards, smallest, largest):
    loudness = 1.0
    for dim, blocks in shards:
        heights = jax.random.uniform(jax.random.fold_in(jax.random.fold_in(stream_key, 6), dim), (blocks,), jnp.float32, smallest / len(shards), largest / len(shards))
        loudness = loudness * jnp.repeat(jnp.exp(heights), shape[dim] // blocks).reshape((-1,) + (1,) * (len(shape) - 1 - dim))
    return loudness


def noise(key, dims, spread, limit, cuts=(), dtype=jnp.bfloat16):
    drawn = jax.random.normal(key, dims, jnp.float32) * spread
    if len(cuts) > 0:
        drawn = shard_levels(key, dims, cuts, -0.22, 0.18) * drawn
    return jnp.clip(drawn, min=-limit, max=limit).astype(dtype)


def setup_inputs(seed: int = 0) -> dict:
    key_list = jax.random.split(jax.random.key(seed), 6)
    return {
        "gradient": noise(key_list[0], (MATS, D, D), 1.0, 6.0, ((0, 2), (1, 8), (2, 8))),
        "left_basis": noise(key_list[1], (MATS, D, D), D ** -0.5, 0.078125, ((0, 2), (1, 8), (2, 8))),
        "right_basis": noise(key_list[2], (MATS, D, D), D ** -0.5, 0.078125, ((0, 2), (1, 8), (2, 8))),
        "first_moment": noise(key_list[3], (MATS, D, D), 1.0, 6.0, ((0, 2), (1, 8), (2, 8)), jnp.float32),
        "second_moment": jnp.clip(jnp.exp(math.log(10.0) - 4.6051702 * jax.random.uniform(key_list[4], (MATS, D, D), jnp.float32) ** shard_levels(key_list[4], (MATS, D, D), ((0, 2), (1, 8), (2, 8)), -0.2, 0.2)), 0.1, 10.0),
    }


beta_value = 0.95
bias_fix = 1.0 - 0.95 ** 10
eps_value = 1e-08

def rounded(x):
    return lax.optimization_barrier(x.astype(jnp.bfloat16)).astype(jnp.float32)

def product(a, b):
    return jnp.dot(a, b, precision=lax.Precision.HIGHEST, preferred_element_type=jnp.float32)

def one_matrix(grad, left, right, first, second):
    grad = grad.astype(jnp.float32)
    left = left.astype(jnp.float32)
    right = right.astype(jnp.float32)
    rotated_left = rounded(product(left.T, grad))
    colb = D // N_COL
    rotated = jnp.zeros((D, D), jnp.float32)
    for block in range(N_COL):
        lower = block * colb
        rotated = rotated + rounded(product(rotated_left[:, lower:lower + colb], right[lower:lower + colb, :]))
    new_first = beta_value * first + (1.0 - beta_value) * rotated
    new_second = beta_value * second + (1.0 - beta_value) * rotated * rotated
    normalized = rounded(new_first / bias_fix / (jnp.sqrt(new_second / bias_fix) + eps_value))
    back_right = rounded(product(normalized, right.T))
    rowb = D // N_ROW
    update = jnp.zeros((D, D), jnp.float32)
    for block in range(N_ROW):
        lower = block * rowb
        update = update + rounded(product(left[:, lower:lower + rowb], back_right[lower:lower + rowb, :]))
    return (update.astype(jnp.bfloat16), new_first, new_second)

def reference(gradient, left_basis, right_basis, first_moment, second_moment):
    updates, firsts, seconds = ([], [], [])
    for index in range(MATS):
        result = one_matrix(gradient[index], left_basis[index], right_basis[index], first_moment[index], second_moment[index])
        updates.append(result[0])
        firsts.append(result[1])
        seconds.append(result[2])
    return (jnp.stack(updates), jnp.stack(firsts), jnp.stack(seconds))
```

```python
import functools
import jax
import jax.numpy as jnp
from jax import lax
from jax.sharding import PartitionSpec as P

beta_value = 0.95
bias_fix = 1.0 - 0.95**10
eps_value = 1e-08

AXES = ("row", "col", "mat")
RING, PAIR = 4, 2
S0, S1, S2, S3 = (0, 0), (1, 0), (2, 0), (3, 0)
O0, O1, O2, O3 = (0, 1), (1, 1), (2, 1), (3, 1)


def split_index(axis, index):
    return (index // PAIR, index % PAIR) if axis == "row" else (index % RING, index // RING)


def join_index(axis, ring, pair):
    return ring * PAIR + pair if axis == "row" else pair * RING + ring


def pairs(axes, move):
    out = []
    for row in range(8):
        for col in range(8):
            for mat in range(2):
                axis = axes[mat]
                if axis is None:
                    continue
                ring, pair = split_index(axis, row if axis == "row" else col)
                ring, pair = ((ring + move) % RING, pair) if move else (ring, 1 - pair)
                there = join_index(axis, ring, pair)
                to = (there, col) if axis == "row" else (row, there)
                out.append(((row * 8 + col) * 2 + mat, (to[0] * 8 + to[1]) * 2 + mat))
    return out


def send(value, axes, move):
    return lax.ppermute(value, AXES, pairs(axes, move))


def member(axes, place):
    found = []
    for axis in axes:
        ring, pair = split_index(axis, lax.axis_index(axis))
        found.append(join_index(axis, (ring + place[0]) % RING, (pair + place[1]) % PAIR))
    return jnp.where(lax.axis_index("mat") == 0, found[0], found[1])


def dot(a, b, da, db):
    return lax.dot_general(a, b, (((da,), (db,)), ((), ())), preferred_element_type=jnp.float32)


def half(x):
    return x.astype(jnp.bfloat16)


def gather(own, axes):
    stack = jnp.zeros((8,) + own.shape, own.dtype)

    def put(stack, place, value):
        return lax.dynamic_update_slice(stack, value[None], (member(axes, place), 0, 0))

    up, down, across = send(own, axes, 1), send(own, axes, -1), send(own, axes, 0)
    stack = put(stack, S0, own)
    up1, down1 = send(across, axes, 1), send(across, axes, -1)
    stack = put(put(put(stack, S3, up), S1, down), O0, across)
    up2, down2 = send(up, axes, 1), send(down1, axes, -1)
    stack = put(put(stack, O3, up1), O1, down1)
    return put(put(stack, S2, up2), O2, down2)


def both(axes, gathers, own, term, weigh):
    gathering = lax.axis_index("mat") == gathers
    at = functools.partial(member, axes)
    one = tuple(a if m == gathers else None for m, a in enumerate(axes))
    other = tuple(a if m != gathers else None for m, a in enumerate(axes))

    def pick(block, summed):
        return jnp.where(gathering, block, half(summed))

    up = send(pick(own, term(at(O2))), axes, 1)
    down = send(pick(own, term(at(S2))), axes, -1)
    across = send(own, one, 0)
    total = weigh(own, at(S0))
    up1 = send(pick(across, term(at(O1)) + up.astype(jnp.float32)), axes, 1)
    down1 = send(pick(across, term(at(O3))), axes, -1)
    total = total + weigh(up, at(S3)) + weigh(down, at(S1)) + weigh(across, at(O0))
    over = send(half(term(at(O0)) + up1.astype(jnp.float32) + down1.astype(jnp.float32)), other, 0)
    up2 = send(pick(up, term(at(S1))), axes, 1)
    down2 = send(pick(down1, term(at(S3)) + down.astype(jnp.float32)), axes, -1)
    total = total + weigh(up1, at(O3)) + weigh(down1, at(O1))
    total = total + weigh(up2, at(S2)) + weigh(down2, at(O2))
    summed = term(at(S0)) + up2.astype(jnp.float32) + down2.astype(jnp.float32) + over.astype(jnp.float32)
    return total, summed


def shards(gradient, left_basis, right_basis, first_moment, second_moment):
    grad, left, right = gradient[0], left_basis[0], right_basis[0]
    first = lax.axis_index("mat") == 0
    a, b = ("col", "row"), ("row", "col")

    def block(stack, index):
        return lax.dynamic_index_in_dim(stack, index, 0, keepdims=False)

    one = gather(jnp.where(first, left, right), a)
    two = gather(jnp.where(first, right, left), b)
    total, summed = both(
        b, 0, grad,
        lambda k: dot(grad, block(one, k), 1, 0),
        lambda x, k: dot(block(one, k), x, 0, 0),
    )
    middle = half(jnp.where(first, total, summed))
    total, summed = both(
        a, 1, middle,
        lambda k: dot(middle, block(two, k), 1, 0),
        lambda x, k: dot(block(two, k), x, 0, 0),
    )
    rotated = jnp.where(first, summed, total)
    new_first = beta_value * first_moment[0] + (1.0 - beta_value) * rotated
    new_second = beta_value * second_moment[0] + (1.0 - beta_value) * rotated * rotated
    normalized = half(new_first / bias_fix / (jnp.sqrt(new_second / bias_fix) + eps_value))
    total, summed = both(
        a, 0, normalized,
        lambda k: dot(block(two, k), normalized, 1, 0),
        lambda x, k: dot(x, block(two, k), 1, 1),
    )
    middle = half(jnp.where(first, total, summed))
    total, summed = both(
        b, 1, middle,
        lambda k: dot(block(one, k), middle, 1, 0),
        lambda x, k: dot(x, block(one, k), 1, 1),
    )
    update = half(jnp.where(first, summed, total))
    return update[None], new_first[None], new_second[None]


def solution(mesh):
    placed = (
        P("mat", "row", "col"),
        P("mat", "col", "row"),
        P("mat", "col", "row"),
        P("mat", "row", "col"),
        P("mat", "row", "col"),
    )
    return jax.shard_map(
        shards,
        mesh=mesh,
        in_specs=placed,
        out_specs=(P("mat", "row", "col"), P("mat", "row", "col"), P("mat", "row", "col")),
        check_vma=False,
    )
```

```python
import functools
import jax
import jax.numpy as jnp
from jax import lax
from jax.experimental import pallas as pl
from jax.experimental.pallas import tpu as pltpu
from jax.sharding import PartitionSpec as P

beta_value = 0.95
bias_fix = 1.0 - 0.95**10
eps_value = 1e-08

AXES = ("row", "col", "mat")
RING, PAIR = 4, 2
S0, S1, S2, S3 = (0, 0), (1, 0), (2, 0), (3, 0)
O0, O1, O2, O3 = (0, 1), (1, 1), (2, 1), (3, 1)
PLACES = (S0, S1, S2, S3, O0, O1, O2, O3)
f32, bf16 = jnp.float32, jnp.bfloat16


def split_index(axis, index):
    return (index // PAIR, index % PAIR) if axis == "row" else (index % RING, index // RING)


def join_index(axis, ring, pair):
    return ring * PAIR + pair if axis == "row" else pair * RING + ring


def pairs(axes, move):
    out = []
    for row in range(8):
        for col in range(8):
            for mat in range(2):
                axis = axes[mat]
                if axis is None:
                    continue
                ring, pair = split_index(axis, row if axis == "row" else col)
                ring, pair = ((ring + move) % RING, pair) if move else (ring, 1 - pair)
                there = join_index(axis, ring, pair)
                to = (there, col) if axis == "row" else (row, there)
                out.append(((row * 8 + col) * 2 + mat, (to[0] * 8 + to[1]) * 2 + mat))
    return out


def send(value, axes, move):
    return lax.ppermute(value, AXES, pairs(axes, move))


def member(axes, place):
    found = []
    for axis in axes:
        ring, pair = split_index(axis, lax.axis_index(axis))
        found.append(join_index(axis, (ring + place[0]) % RING, (pair + place[1]) % PAIR))
    return jnp.where(lax.axis_index("mat") == 0, found[0], found[1])


def chunks(n):
    return [slice(i, min(i + 256, n)) for i in range(0, n, 256)]


def call(body, outs, *args, flops=0, scratch=()):
    vmem = pl.BlockSpec(memory_space=pltpu.VMEM)
    return pl.pallas_call(
        body,
        out_shape=outs,
        in_specs=[pl.BlockSpec(memory_space=pltpu.SMEM)] + [vmem] * (len(args) - 1),
        out_specs=[vmem] * len(outs),
        scratch_shapes=scratch,
        compiler_params=pltpu.CompilerParams(vmem_limit_bytes=VMEM_LIMIT),
        cost_estimate=pl.CostEstimate(flops=flops, bytes_accessed=0, transcendentals=0),
    )(*args)


VMEM_LIMIT = 20 * 2**20


def write_term(scalars, weights, own, place, out):
    index = scalars[1 + PLACES.index(place)]
    for n in chunks(out.shape[1]):
        out[:, n] = jnp.dot(own[...], weights[index, :, n], preferred_element_type=f32).astype(bf16)


def weighed(scalars, weights, blocks, n):
    total = None
    for place, block in blocks:
        index = scalars[1 + PLACES.index(place)]
        part = jnp.dot(weights[index], block[:, n], preferred_element_type=f32)
        total = part if total is None else total + part
    return total


def both(axes, gathers, scalars, weights, own, finish, extra, outs):
    mine = lax.axis_index("mat") == gathers
    scalars = jnp.concatenate([mine.astype(jnp.int32)[None], scalars])
    one = tuple(a if m == gathers else None for m, a in enumerate(axes))
    other = tuple(a if m != gathers else None for m, a in enumerate(axes))
    n = own.shape[1]
    block = jax.ShapeDtypeStruct(own.shape, bf16)
    acc = jax.ShapeDtypeStruct((n, n), f32)
    cost = 2 * n**3

    def open_body(s, w, a, u, d):
        @pl.when(s[0] == 1)
        def _():
            u[...] = a[...]
            d[...] = a[...]

        @pl.when(s[0] == 0)
        def _():
            write_term(s, w, a, O2, u)
            write_term(s, w, a, S2, d)

    u, d = call(open_body, [block] * 2, scalars, weights, own, flops=2 * cost)
    across, up, down = send(own, one, 0), send(u, axes, 1), send(d, axes, -1)

    kept = (O1, O3, O0, S1, S3, S0)

    def terms_body(s, w, a, *out):
        @pl.when(s[0] == 0)
        def _():
            for place, o in zip(kept, out, strict=True):
                write_term(s, w, a, place, o)

    term = dict(zip(kept, call(terms_body, [block] * 6, scalars, weights, own, flops=6 * cost), strict=True))

    def step1_body(s, c, u, p1, p3, ou, od):
        @pl.when(s[0] == 1)
        def _():
            ou[...] = c[...]
            od[...] = c[...]

        @pl.when(s[0] == 0)
        def _():
            ou[...] = (p1[...].astype(f32) + u[...].astype(f32)).astype(bf16)
            od[...] = p3[...]

    u, d = call(step1_body, [block] * 2, scalars, across, up, term[O1], term[O3])
    up1, down1 = send(u, axes, 1), send(d, axes, -1)

    def weigh1_body(s, w, o, u, d, c, out):
        @pl.when(s[0] == 1)
        def _():
            for k in chunks(n):
                out[:, k] = weighed(s, w, ((S0, o), (S3, u), (S1, d), (O0, c)), k)

    total = call(weigh1_body, [acc], scalars, weights, own, up, down, across, flops=4 * cost)[0]

    def step2_body(s, u, d, u1, d1, p0, q1, q3, oo, ou, od):
        @pl.when(s[0] == 1)
        def _():
            ou[...] = u[...]
            od[...] = d1[...]

        @pl.when(s[0] == 0)
        def _():
            oo[...] = (p0[...].astype(f32) + u1[...].astype(f32) + d1[...].astype(f32)).astype(bf16)
            ou[...] = q1[...]
            od[...] = (q3[...].astype(f32) + d[...].astype(f32)).astype(bf16)

    o, u, d = call(step2_body, [block] * 3, scalars, up, down, up1, down1, term[O0], term[S1], term[S3])
    over, up2, down2 = send(o, other, 0), send(u, axes, 1), send(d, axes, -1)

    def weigh2_body(s, w, t, u, d, out):
        @pl.when(s[0] == 1)
        def _():
            for k in chunks(n):
                out[:, k] = t[:, k] + weighed(s, w, ((O3, u), (O1, d)), k)

    total = call(weigh2_body, [acc], scalars, weights, total, up1, down1, flops=2 * cost)[0]

    def last_body(s, w, t, p, u, d, c, *refs):
        more, out, scratch = refs[: len(extra)], refs[len(extra) : len(extra) + len(outs)], refs[-1]

        @pl.when(s[0] == 1)
        def _():
            for k in chunks(n):
                scratch[:, k] = t[:, k] + weighed(s, w, ((S2, u), (O2, d)), k)

        @pl.when(s[0] == 0)
        def _():
            parts = [x[...].astype(f32) for x in (p, u, d, c)]
            scratch[...] = (parts[0] + parts[1]) + (parts[2] + parts[3])

        finish(scratch, more, out)

    return call(
        last_body, outs, scalars, weights, total, term[S0], up2, down2, over, *extra,
        flops=2 * cost, scratch=[pltpu.VMEM((n, n), f32)],
    )


def gather(own, axes, scalars):
    across, up, down = send(own, axes, 0), send(own, axes, 1), send(own, axes, -1)
    up1, down1 = send(across, axes, 1), send(across, axes, -1)
    up2, down2 = send(up, axes, 1), send(down1, axes, -1)

    def body(s, *refs):
        for i, ref in enumerate(refs[:-1]):
            refs[-1][s[i]] = ref[...]

    out = jax.ShapeDtypeStruct((8,) + own.shape, own.dtype)
    return call(body, [out], scalars, own, down, up2, up, across, down1, down2, up1)[0]


def to_block(total, more, out):
    out[0][...] = total[...].astype(bf16)


def moments(total, more, out):
    n = total.shape[0]
    for k in [slice(i, i + n // 5) for i in range(0, n, n // 5)]:
        rotated = total[:, k]
        first = beta_value * more[0][:, k] + (1.0 - beta_value) * rotated
        second = beta_value * more[1][:, k] + (1.0 - beta_value) * rotated * rotated
        out[0][:, k] = first
        out[1][:, k] = second
        quotient = first / bias_fix / (jnp.sqrt(second / bias_fix) + eps_value)
        out[2][k, :] = quotient.astype(bf16).T


def turned(total, more, out):
    out[0][...] = total[...].astype(bf16).T


def place_body(s, left, right, one, two):
    @pl.when(s[0] == 0)
    def _():
        one[...] = left[...].T
        two[...] = right[...]

    @pl.when(s[0] == 1)
    def _():
        one[...] = right[...]
        two[...] = left[...].T


def shards(gradient, left_basis, right_basis, first_moment, second_moment):
    grad, left, right = gradient[0], left_basis[0], right_basis[0]
    a, b = ("col", "row"), ("row", "col")
    at_a, at_b = (jnp.stack([member(axes, p) for p in PLACES]).astype(jnp.int32) for axes in (a, b))
    n = grad.shape[0]
    block, whole = jax.ShapeDtypeStruct((n, n), bf16), jax.ShapeDtypeStruct((n, n), f32)
    one, two = call(place_body, [block] * 2, lax.axis_index("mat").astype(jnp.int32)[None], left, right)
    one, two = gather(one, a, at_a), gather(two, b, at_b)
    (middle,) = both(b, 0, at_b, one, grad, to_block, (), [block])
    new_first, new_second, normalized = both(
        a, 1, at_a, two, middle, moments, (first_moment[0], second_moment[0]), [whole, whole, block]
    )
    (middle,) = both(a, 0, at_a, two, normalized, to_block, (), [block])
    (update,) = both(b, 1, at_b, one, middle, turned, (), [block])
    return update[None], new_first[None], new_second[None]


def solution(mesh):
    placed = (
        P("mat", "row", "col"),
        P("mat", "col", "row"),
        P("mat", "col", "row"),
        P("mat", "row", "col"),
        P("mat", "row", "col"),
    )
    return jax.shard_map(
        shards,
        mesh=mesh,
        in_specs=placed,
        out_specs=(P("mat", "row", "col"), P("mat", "row", "col"), P("mat", "row", "col")),
        check_vma=False,
    )
```

```python
import functools
import jax
import jax.numpy as jnp
from jax import lax
from jax.experimental import pallas as pl
from jax.experimental.pallas import tpu as pltpu
from jax.sharding import PartitionSpec as P

beta_value = 0.95
bias_fix = 1.0 - 0.95**10
eps_value = 1e-08

AXES = ("row", "col", "mat")
RING, PAIR = 4, 2
S0, S1, S2, S3 = (0, 0), (1, 0), (2, 0), (3, 0)
O0, O1, O2, O3 = (0, 1), (1, 1), (2, 1), (3, 1)
PLACES = (S0, S1, S2, S3, O0, O1, O2, O3)
f32, bf16 = jnp.float32, jnp.bfloat16


def split_index(axis, index):
    return (index // PAIR, index % PAIR) if axis == "row" else (index % RING, index // RING)


def join_index(axis, ring, pair):
    return ring * PAIR + pair if axis == "row" else pair * RING + ring


def pairs(axes, move):
    out = []
    for row in range(8):
        for col in range(8):
            for mat in range(2):
                axis = axes[mat]
                if axis is None:
                    continue
                ring, pair = split_index(axis, row if axis == "row" else col)
                ring, pair = ((ring + move) % RING, pair) if move else (ring, 1 - pair)
                there = join_index(axis, ring, pair)
                to = (there, col) if axis == "row" else (row, there)
                out.append(((row * 8 + col) * 2 + mat, (to[0] * 8 + to[1]) * 2 + mat))
    return out


def send(value, axes, move):
    return lax.ppermute(value, AXES, pairs(axes, move))


def member(axes, place):
    found = []
    for axis in axes:
        ring, pair = split_index(axis, lax.axis_index(axis))
        found.append(join_index(axis, (ring + place[0]) % RING, (pair + place[1]) % PAIR))
    return jnp.where(lax.axis_index("mat") == 0, found[0], found[1]).astype(jnp.int32)


def chunks(n):
    return [slice(i, min(i + 256, n)) for i in range(0, n, 256)]


def stay(x):
    return pltpu.with_memory_space_constraint(x, pltpu.VMEM)


def leave_out(x):
    return pltpu.with_memory_space_constraint(x, pltpu.HBM)


def kept_array(x):
    return pltpu.VMEM(x.shape, x.dtype)


def call(body, outs, *args, flops=0, scratch=(), after=(), leave=0, loose=0):
    vmem, place = pl.BlockSpec(memory_space=pltpu.VMEM), pl.BlockSpec(memory_space=pl.ANY)
    inputs = len(args)
    held = sum(x.size * x.dtype.itemsize for x in (*args[1:], *outs[:leave], *scratch) if x.ndim == 2)

    def whole(*refs):
        body(*refs[:inputs], *refs[inputs + len(after) :])

    return pl.pallas_call(
        whole,
        out_shape=[x if i < leave else kept_array(x) for i, x in enumerate(outs)],
        in_specs=[pl.BlockSpec(memory_space=pltpu.SMEM)] + [vmem] * (inputs - 1) + [place] * len(after),
        out_specs=[vmem] * len(outs),
        scratch_shapes=[pltpu.VMEM(x.shape, x.dtype) for x in scratch],
        compiler_params=pltpu.CompilerParams(vmem_limit_bytes=held + 4 * 2**20),
        cost_estimate=pl.CostEstimate(flops=flops, bytes_accessed=0, transcendentals=0),
    )(args[0], *[x if i < loose else stay(x) for i, x in enumerate(args[1:])], *after)


def block_of(scalars, place):
    return scalars[1 + PLACES.index(place)]


def write_term(own, w, index, out):
    for n in chunks(out.shape[1]):
        out[:, n] = jnp.dot(own[...], w[index, :, n], preferred_element_type=f32).astype(bf16)


def weighed(s, w, pairs, n):
    parts = [jnp.dot(w[block_of(s, p)], x[:, n], preferred_element_type=f32) for p, x in pairs]
    while len(parts) > 1:
        parts = [a + b for a, b in zip(parts[0::2], parts[1::2], strict=True)]
    return parts[0]


def write_first(s, w, own, u, d):
    @pl.when(s[0] == 1)
    def _():
        u[...] = own[...]
        d[...] = own[...]

    @pl.when(s[0] == 0)
    def _():
        write_term(own, w, block_of(s, O2), u)
        write_term(own, w, block_of(s, S2), d)


def both(axes, gathers, scalars, weights, own, first, finish, extra, outs, leave=0, following=None, early=(), late=()):
    one = tuple(a if m == gathers else None for m, a in enumerate(axes))
    other = tuple(a if m != gathers else None for m, a in enumerate(axes))
    n = own.shape[1]
    block = jax.ShapeDtypeStruct(own.shape, bf16)
    acc = jax.ShapeDtypeStruct((n, n), f32)
    cost = 2 * n**3
    u, d = first
    across, up, down = send(own, one, 0), send(u, axes, 1), send(d, axes, -1)

    kept = (O1, O3, O0, S1, S3, S0)

    def terms_body(s, w, a, *out):
        @pl.when(s[0] == 0)
        def _():
            for place, o in zip(kept, out, strict=True):
                write_term(a, w, block_of(s, place), o)

    term = dict(zip(kept, call(terms_body, [block] * 6, scalars, weights, own, flops=6 * cost), strict=True))

    def step1_body(s, c, u, p1, p3, ou, od):
        @pl.when(s[0] == 1)
        def _():
            ou[...] = c[...]
            od[...] = c[...]

        @pl.when(s[0] == 0)
        def _():
            ou[...] = (p1[...].astype(f32) + u[...].astype(f32)).astype(bf16)
            od[...] = p3[...]

    u, d = call(step1_body, [block] * 2, scalars, across, up, term[O1], term[O3], after=early)
    up1, down1 = send(u, axes, 1), send(d, axes, -1)

    def weigh1_body(s, w, o, u, d, c, out):
        @pl.when(s[0] == 1)
        def _():
            for k in chunks(n):
                out[:, k] = weighed(s, w, ((S0, o), (S3, u), (S1, d), (O0, c)), k)

    total = call(weigh1_body, [acc], scalars, weights, own, up, down, across, flops=4 * cost)[0]

    def step2_body(s, u, d, u1, d1, p0, q1, q3, oo, ou, od):
        @pl.when(s[0] == 1)
        def _():
            ou[...] = u[...]
            od[...] = d1[...]

        @pl.when(s[0] == 0)
        def _():
            oo[...] = (p0[...].astype(f32) + u1[...].astype(f32) + d1[...].astype(f32)).astype(bf16)
            ou[...] = q1[...]
            od[...] = (q3[...].astype(f32) + d[...].astype(f32)).astype(bf16)

    o, u, d = call(
        step2_body, [block] * 3, scalars, up, down, up1, down1, term[O0], term[S1], term[S3], after=(total, *late)
    )
    over, up2, down2 = send(o, other, 0), send(u, axes, 1), send(d, axes, -1)

    def weigh2_body(s, w, t, u, d, p, c, out):
        @pl.when(s[0] == 1)
        def _():
            for k in chunks(n):
                out[:, k] = t[:, k] + weighed(s, w, ((O3, u), (O1, d)), k)

        @pl.when(s[0] == 0)
        def _():
            out[...] = p[...].astype(f32) + c[...].astype(f32)

    total = call(weigh2_body, [acc], scalars, weights, total, up1, down1, term[S0], over, flops=2 * cost)[0]
    ahead = [] if following is None else following
    opened = [block] * len(ahead)

    def last_body(s, w, t, u, d, *refs):
        then, refs = refs[: len(ahead)], refs[len(ahead) :]
        more, refs = refs[: len(extra)], refs[len(extra) :]
        out, begin, scratch = refs[: len(outs)], refs[len(outs) : -1], refs[-1]

        @pl.when(s[0] == 1)
        def _():
            for k in chunks(n):
                scratch[:, k] = t[:, k] + weighed(s, w, ((S2, u), (O2, d)), k)

        @pl.when(s[0] == 0)
        def _():
            scratch[...] = t[...] + (u[...].astype(f32) + d[...].astype(f32))

        finish(scratch, more, out)
        if ahead:
            write_first(*then, out[-1], *begin)

    return call(
        last_body, [*outs, *opened], scalars, weights, total, up2, down2, *ahead, *extra,
        flops=2 * cost, scratch=[acc], leave=leave,
    )


def stacked(scalars, blocks, after=(), far=False):
    flat = [x for block in blocks for x in (block if isinstance(block, tuple) else (block,))]
    n = flat[0].shape[1]

    def body(s, *refs):
        out, sems, copies, at = refs[-2], refs[-1], [], 0
        for place, block in zip(PLACES, blocks, strict=True):
            row = 0
            for x in block if isinstance(block, tuple) else (block,):
                target = out.at[block_of(s, place), pl.ds(row, x.shape[0])]
                copies.append(pltpu.make_async_copy(refs[at], target, sems.at[at]))
                row += x.shape[0]
                at += 1
        for copy in copies:
            copy.start()
        for copy in copies:
            copy.wait()

    place = pl.BlockSpec(memory_space=pl.ANY)
    return pl.pallas_call(
        lambda s, *refs: body(s, *refs[: len(flat)], *refs[len(flat) + len(after) :]),
        out_shape=kept_array(jax.ShapeDtypeStruct((8, n, n), bf16)),
        in_specs=[pl.BlockSpec(memory_space=pltpu.SMEM)] + [place] * (len(flat) + len(after)),
        out_specs=pl.BlockSpec(memory_space=pltpu.VMEM),
        scratch_shapes=[pltpu.SemaphoreType.DMA((len(flat),))],
        compiler_params=pltpu.CompilerParams(vmem_limit_bytes=4 * 2**20),
        cost_estimate=pl.CostEstimate(flops=0, bytes_accessed=2 * 8 * n * n * 2, transcendentals=0),
    )(scalars, *[leave_out(x) if far else x for x in flat], *after)


def tied(scalars, value, after):
    def body(s, x, o):
        o[...] = x[...]

    return call(body, [jax.ShapeDtypeStruct(value.shape, value.dtype)], scalars, value, after=after)[0]


def to_block(total, more, out):
    out[0][...] = total[...].astype(bf16)


def moments(total, more, out):
    n = total.shape[0]
    for k in [slice(i, i + n // 5) for i in range(0, n, n // 5)]:
        rotated = total[:, k]
        first = beta_value * more[0][:, k] + (1.0 - beta_value) * rotated
        second = beta_value * more[1][:, k] + (1.0 - beta_value) * rotated * rotated
        out[0][:, k] = first
        out[1][:, k] = second
        quotient = first / bias_fix / (jnp.sqrt(second / bias_fix) + eps_value)
        out[2][k, :] = quotient.astype(bf16).T


def turned(total, more, out):
    out[0][...] = total[...].astype(bf16).T


def place_body(s, left, right, one, two):
    @pl.when(s[0] == 0)
    def _():
        one[...] = left[...].T
        two[...] = right[...]

    @pl.when(s[0] == 1)
    def _():
        one[...] = right[...]
        two[...] = left[...].T


def shards(gradient, left_basis, right_basis, first_moment, second_moment):
    grad, left, right = gradient[0], left_basis[0], right_basis[0]
    mat = lax.axis_index("mat").astype(jnp.int32)
    a, b = ("col", "row"), ("row", "col")

    def scalars(gathers, axes):
        return jnp.stack([mat if gathers else 1 - mat] + [member(axes, p) for p in PLACES])

    slot2, slot4, slot5, slot6 = scalars(0, b), scalars(1, a), scalars(0, a), scalars(1, b)
    n = grad.shape[0]
    block, whole = jax.ShapeDtypeStruct((n, n), bf16), jax.ShapeDtypeStruct((n, n), f32)
    one, two = call(place_body, [block] * 2, mat[None], left, right, loose=2)

    across, up, down = send(one, a, 0), send(one, a, 1), send(one, a, -1)
    downb = send(two, b, -1)
    relay = tied(slot2, across, (up, down, downb))
    up1, down1, up2 = send(relay, a, 1), send(relay, a, -1), send(up, a, 1)
    acrossb = send(tied(slot2, two, (relay,)), b, 0)
    down2 = send(down1, a, -1)
    upb = send(tied(slot2, two, (down1,)), b, 1)
    gathered_a = (one, down, up2, up, across, down1, down2, up1)
    weights_a = stacked(slot5, gathered_a)

    first = call(write_first, [block] * 2, slot2, weights_a, grad, flops=4 * n**3)
    upb1, downb1 = send(acrossb, b, 1), send(acrossb, b, -1)
    upb2 = send(upb, b, 1)
    downb2 = send(downb1, b, -1)
    weights_b = stacked(slot2, (two, downb, upb2, upb, acrossb, downb1, downb2, upb1))
    middle, *first = both(
        b, 0, slot2, weights_a, grad, first, to_block, (), [block], 0, (slot4, weights_b), (upb,),
        (upb2, downb1),
    )
    new_first, new_second, normalized, *first = both(
        a, 1, slot4, weights_b, middle, first, moments, (first_moment[0], second_moment[0]), [whole, whole, block],
        2, (slot5, weights_b),
    )
    weights_a = stacked(slot5, gathered_a, (normalized,), True)
    middle, *first = both(
        a, 0, slot5, weights_b, normalized, first, to_block, (), [block], 0, (slot6, weights_a), (), (weights_a,)
    )
    (update,) = both(b, 1, slot6, weights_a, middle, first, turned, (), [block], 1)
    return update[None], new_first[None], new_second[None]


def solution(mesh):
    placed = (
        P("mat", "row", "col"),
        P("mat", "col", "row"),
        P("mat", "col", "row"),
        P("mat", "row", "col"),
        P("mat", "row", "col"),
    )
    return jax.shard_map(
        shards,
        mesh=mesh,
        in_specs=placed,
        out_specs=(P("mat", "row", "col"), P("mat", "row", "col"), P("mat", "row", "col")),
        check_vma=False,
    )
```

```python
import functools
import jax
import jax.numpy as jnp
from jax import lax
from jax.experimental import pallas as pl
from jax.experimental.pallas import tpu as pltpu
from jax.sharding import PartitionSpec as P

beta_value = 0.95
bias_fix = 1.0 - 0.95**10
eps_value = 1e-08

AXES = ("row", "col", "mat")
RING, PAIR = 4, 2
S0, S1, S2, S3 = (0, 0), (1, 0), (2, 0), (3, 0)
O0, O1, O2, O3 = (0, 1), (1, 1), (2, 1), (3, 1)
PLACES = (S0, S1, S2, S3, O0, O1, O2, O3)
f32, bf16 = jnp.float32, jnp.bfloat16


def split_index(axis, index):
    return (index // PAIR, index % PAIR) if axis == "row" else (index % RING, index // RING)


def join_index(axis, ring, pair):
    return ring * PAIR + pair if axis == "row" else pair * RING + ring


def pairs(axes, move):
    out = []
    for row in range(8):
        for col in range(8):
            for mat in range(2):
                axis = axes[mat]
                if axis is None:
                    continue
                ring, pair = split_index(axis, row if axis == "row" else col)
                ring, pair = ((ring + move) % RING, pair) if move else (ring, 1 - pair)
                there = join_index(axis, ring, pair)
                to = (there, col) if axis == "row" else (row, there)
                out.append(((row * 8 + col) * 2 + mat, (to[0] * 8 + to[1]) * 2 + mat))
    return out


def send(value, axes, move):
    return lax.ppermute(value, AXES, pairs(axes, move))


def member(axes, place):
    found = []
    for axis in axes:
        ring, pair = split_index(axis, lax.axis_index(axis))
        found.append(join_index(axis, (ring + place[0]) % RING, (pair + place[1]) % PAIR))
    return jnp.where(lax.axis_index("mat") == 0, found[0], found[1]).astype(jnp.int32)


def chunks(n):
    return [slice(i, min(i + 256, n)) for i in range(0, n, 256)]


def stay(x):
    return pltpu.with_memory_space_constraint(x, pltpu.VMEM)


def leave_out(x):
    return pltpu.with_memory_space_constraint(x, pltpu.HBM)


def kept_array(x):
    return pltpu.VMEM(x.shape, x.dtype)


def call(body, outs, *args, flops=0, scratch=(), after=(), leave=0, loose=0):
    vmem, place = pl.BlockSpec(memory_space=pltpu.VMEM), pl.BlockSpec(memory_space=pl.ANY)
    inputs = len(args)
    held = sum(x.size * x.dtype.itemsize for x in (*args[1:], *outs[:leave], *scratch) if x.ndim == 2)

    def whole(*refs):
        body(*refs[:inputs], *refs[inputs + len(after) :])

    return pl.pallas_call(
        whole,
        out_shape=[x if i < leave else kept_array(x) for i, x in enumerate(outs)],
        in_specs=[pl.BlockSpec(memory_space=pltpu.SMEM)] + [vmem] * (inputs - 1) + [place] * len(after),
        out_specs=[vmem] * len(outs),
        scratch_shapes=[pltpu.VMEM(x.shape, x.dtype) for x in scratch],
        compiler_params=pltpu.CompilerParams(vmem_limit_bytes=held + 4 * 2**20),
        cost_estimate=pl.CostEstimate(flops=flops, bytes_accessed=0, transcendentals=0),
    )(args[0], *[x if i < loose else stay(x) for i, x in enumerate(args[1:])], *after)


def block_of(scalars, place):
    return scalars[1 + PLACES.index(place)]


def write_term(own, w, index, out):
    for n in chunks(out.shape[1]):
        out[:, n] = jnp.dot(own[...], w[index, :, n], preferred_element_type=f32).astype(bf16)


def weighed(s, w, pairs, n):
    parts = [jnp.dot(w[block_of(s, p)], x[:, n], preferred_element_type=f32) for p, x in pairs]
    while len(parts) > 1:
        parts = [a + b for a, b in zip(parts[0::2], parts[1::2], strict=True)]
    return parts[0]


def write_first(s, w, own, u, d):
    @pl.when(s[0] == 1)
    def _():
        u[...] = own[...]
        d[...] = own[...]

    @pl.when(s[0] == 0)
    def _():
        write_term(own, w, block_of(s, O2), u)
        write_term(own, w, block_of(s, S2), d)


def both(axes, gathers, scalars, weights, own, first, finish, extra, outs, leave=0, following=None, early=(), late=()):
    one = tuple(a if m == gathers else None for m, a in enumerate(axes))
    other = tuple(a if m != gathers else None for m, a in enumerate(axes))
    n = own.shape[1]
    block = jax.ShapeDtypeStruct(own.shape, bf16)
    acc = jax.ShapeDtypeStruct((n, n), f32)
    cost = 2 * n**3
    u, d = first
    across, up, down = send(own, one, 0), send(u, axes, 1), send(d, axes, -1)

    kept = (O1, O3, O0, S1, S3, S0)

    def terms_body(s, w, a, *out):
        @pl.when(s[0] == 0)
        def _():
            for place, o in zip(kept, out, strict=True):
                write_term(a, w, block_of(s, place), o)

    term = dict(zip(kept, call(terms_body, [block] * 6, scalars, weights, own, flops=6 * cost), strict=True))

    def step1_body(s, c, u, p1, p3, ou, od):
        @pl.when(s[0] == 1)
        def _():
            ou[...] = c[...]
            od[...] = c[...]

        @pl.when(s[0] == 0)
        def _():
            ou[...] = (p1[...].astype(f32) + u[...].astype(f32)).astype(bf16)
            od[...] = p3[...]

    u, d = call(step1_body, [block] * 2, scalars, across, up, term[O1], term[O3], after=early)
    up1, down1 = send(u, axes, 1), send(d, axes, -1)

    def weigh1_body(s, w, o, u, d, c, out):
        @pl.when(s[0] == 1)
        def _():
            for k in chunks(n):
                out[:, k] = weighed(s, w, ((S0, o), (S3, u), (S1, d), (O0, c)), k)

    total = call(weigh1_body, [acc], scalars, weights, own, up, down, across, flops=4 * cost)[0]

    def step2_body(s, u, d, u1, d1, p0, q1, q3, oo, ou, od):
        @pl.when(s[0] == 1)
        def _():
            ou[...] = u[...]
            od[...] = d1[...]

        @pl.when(s[0] == 0)
        def _():
            oo[...] = (p0[...].astype(f32) + u1[...].astype(f32) + d1[...].astype(f32)).astype(bf16)
            ou[...] = q1[...]
            od[...] = (q3[...].astype(f32) + d[...].astype(f32)).astype(bf16)

    o, u, d = call(
        step2_body, [block] * 3, scalars, up, down, up1, down1, term[O0], term[S1], term[S3], after=(total, *late)
    )
    over, up2, down2 = send(o, other, 0), send(u, axes, 1), send(d, axes, -1)

    def weigh2_body(s, w, t, u, d, p, c, out):
        @pl.when(s[0] == 1)
        def _():
            for k in chunks(n):
                out[:, k] = t[:, k] + weighed(s, w, ((O3, u), (O1, d)), k)

        @pl.when(s[0] == 0)
        def _():
            out[...] = p[...].astype(f32) + c[...].astype(f32)

    total = call(weigh2_body, [acc], scalars, weights, total, up1, down1, term[S0], over, flops=2 * cost)[0]
    ahead = [] if following is None else following
    opened = [block] * len(ahead)

    def last_body(s, w, t, u, d, *refs):
        then, refs = refs[: len(ahead)], refs[len(ahead) :]
        more, refs = refs[: len(extra)], refs[len(extra) :]
        out, begin, scratch = refs[: len(outs)], refs[len(outs) : -1], refs[-1]

        @pl.when(s[0] == 1)
        def _():
            for k in chunks(n):
                scratch[:, k] = t[:, k] + weighed(s, w, ((S2, u), (O2, d)), k)

        @pl.when(s[0] == 0)
        def _():
            scratch[...] = t[...] + (u[...].astype(f32) + d[...].astype(f32))

        finish(scratch, more, out)
        if ahead:
            write_first(*then, out[-1], *begin)

    return call(
        last_body, [*outs, *opened], scalars, weights, total, up2, down2, *ahead, *extra,
        flops=2 * cost, scratch=[acc], leave=leave,
    )


def stacked(scalars, blocks, after=(), far=False):
    flat = [x for block in blocks for x in (block if isinstance(block, tuple) else (block,))]
    n = flat[0].shape[1]

    def body(s, *refs):
        out, sems, copies, at = refs[-2], refs[-1], [], 0
        for place, block in zip(PLACES, blocks, strict=True):
            row = 0
            for x in block if isinstance(block, tuple) else (block,):
                target = out.at[block_of(s, place), pl.ds(row, x.shape[0])]
                copies.append(pltpu.make_async_copy(refs[at], target, sems.at[at]))
                row += x.shape[0]
                at += 1
        for copy in copies:
            copy.start()
        for copy in copies:
            copy.wait()

    place = pl.BlockSpec(memory_space=pl.ANY)
    return pl.pallas_call(
        lambda s, *refs: body(s, *refs[: len(flat)], *refs[len(flat) + len(after) :]),
        out_shape=kept_array(jax.ShapeDtypeStruct((8, n, n), bf16)),
        in_specs=[pl.BlockSpec(memory_space=pltpu.SMEM)] + [place] * (len(flat) + len(after)),
        out_specs=pl.BlockSpec(memory_space=pltpu.VMEM),
        scratch_shapes=[pltpu.SemaphoreType.DMA((len(flat),))],
        compiler_params=pltpu.CompilerParams(vmem_limit_bytes=4 * 2**20),
        cost_estimate=pl.CostEstimate(flops=0, bytes_accessed=2 * 8 * n * n * 2, transcendentals=0),
    )(scalars, *[leave_out(x) if far else x for x in flat], *after)


def tied(value, after=()):
    place = pl.BlockSpec(memory_space=pl.ANY)
    return pl.pallas_call(
        lambda *refs: None,
        out_shape=jax.ShapeDtypeStruct(value.shape, value.dtype),
        in_specs=[place] * (1 + len(after)),
        out_specs=place,
        input_output_aliases={0: 0},
        cost_estimate=pl.CostEstimate(flops=0, bytes_accessed=0, transcendentals=0),
    )(value, *after)


def to_block(total, more, out):
    out[0][...] = total[...].astype(bf16)


def moments(total, more, out):
    n = total.shape[0]
    for k in [slice(i, i + n // 5) for i in range(0, n, n // 5)]:
        rotated = total[:, k]
        first = beta_value * more[0][:, k] + (1.0 - beta_value) * rotated
        second = beta_value * more[1][:, k] + (1.0 - beta_value) * rotated * rotated
        out[0][:, k] = first
        out[1][:, k] = second
        quotient = first / bias_fix / (jnp.sqrt(second / bias_fix) + eps_value)
        out[2][k, :] = quotient.astype(bf16).T


def turned(total, more, out):
    out[0][...] = total[...].astype(bf16).T


def placed_bases(mat, left, right):
    n = left.shape[0]
    block = jax.ShapeDtypeStruct((n, n), bf16)

    def body(s, left, right, one, two, x, y, sems):
        copies = [pltpu.make_async_copy(left, x, sems.at[0]), pltpu.make_async_copy(right, y, sems.at[1])]
        for copy in copies:
            copy.start()
        for copy in copies:
            copy.wait()

        @pl.when(s[0] == 0)
        def _():
            one[...] = x[...].T
            two[...] = y[...]

        @pl.when(s[0] == 1)
        def _():
            one[...] = y[...]
            two[...] = x[...].T

    place, vmem = pl.BlockSpec(memory_space=pl.ANY), pl.BlockSpec(memory_space=pltpu.VMEM)
    return pl.pallas_call(
        body,
        out_shape=[kept_array(block)] * 2,
        in_specs=[pl.BlockSpec(memory_space=pltpu.SMEM), place, place],
        out_specs=[vmem] * 2,
        scratch_shapes=[pltpu.VMEM((n, n), bf16), pltpu.VMEM((n, n), bf16), pltpu.SemaphoreType.DMA((2,))],
        compiler_params=pltpu.CompilerParams(vmem_limit_bytes=8 * 2**20),
        cost_estimate=pl.CostEstimate(flops=0, bytes_accessed=4 * n * n * 2, transcendentals=0),
    )(mat, leave_out(left), leave_out(right))


def shards(gradient, left_basis, right_basis, first_moment, second_moment):
    grad, left, right = gradient[0], left_basis[0], right_basis[0]
    mat = lax.axis_index("mat").astype(jnp.int32)
    a, b = ("col", "row"), ("row", "col")

    def scalars(gathers, axes):
        return jnp.stack([mat if gathers else 1 - mat] + [member(axes, p) for p in PLACES])

    slot2, slot4, slot5, slot6 = scalars(0, b), scalars(1, a), scalars(0, a), scalars(1, b)
    n = grad.shape[0]
    block, whole = jax.ShapeDtypeStruct((n, n), bf16), jax.ShapeDtypeStruct((n, n), f32)
    one, two = placed_bases(mat[None], left, right)

    across, up, down = send(one, a, 0), send(one, a, 1), send(one, a, -1)
    upb, downb = send(two, b, 1), send(two, b, -1)
    relay = tied(tied(across), (up, down, upb, downb))
    up1, down1, up2 = send(relay, a, 1), send(relay, a, -1), send(up, a, 1)
    two = tied(two, (relay,))
    acrossb = send(two, b, 0)
    down2 = send(down1, a, -1)
    gathered_a = (one, down, up2, up, relay, down1, down2, up1)
    weights_a = stacked(slot5, gathered_a)

    first = call(write_first, [block] * 2, slot2, weights_a, grad, flops=4 * n**3)
    upb1, downb1 = send(acrossb, b, 1), send(acrossb, b, -1)
    upb2 = send(upb, b, 1)
    downb2 = send(downb1, b, -1)
    weights_b = stacked(slot2, (two, downb, upb2, upb, acrossb, downb1, downb2, upb1))
    middle, *first = both(
        b, 0, slot2, weights_a, grad, first, to_block, (), [block], 0, (slot4, weights_b), (),
        (upb2, downb1),
    )
    new_first, new_second, normalized, *first = both(
        a, 1, slot4, weights_b, middle, first, moments, (first_moment[0], second_moment[0]), [whole, whole, block],
        2, (slot5, weights_b),
    )
    weights_a = stacked(slot5, gathered_a, (normalized,), True)
    middle, *first = both(
        a, 0, slot5, weights_b, normalized, first, to_block, (), [block], 0, (slot6, weights_a), (), (weights_a,)
    )
    (update,) = both(b, 1, slot6, weights_a, middle, first, turned, (), [block], 1)
    return update[None], new_first[None], new_second[None]


def solution(mesh):
    placed = (
        P("mat", "row", "col"),
        P("mat", "col", "row"),
        P("mat", "col", "row"),
        P("mat", "row", "col"),
        P("mat", "row", "col"),
    )
    return jax.shard_map(
        shards,
        mesh=mesh,
        in_specs=placed,
        out_specs=(P("mat", "row", "col"), P("mat", "row", "col"), P("mat", "row", "col")),
        check_vma=False,
    )
```

```python
import functools
import jax
import jax.numpy as jnp
from jax import lax
from jax.experimental import pallas as pl
from jax.experimental.pallas import tpu as pltpu
from jax.sharding import PartitionSpec as P

beta_value = 0.95
bias_fix = 1.0 - 0.95**10
eps_value = 1e-08

AXES = ("row", "col", "mat")
RING, PAIR = 4, 2
S0, S1, S2, S3 = (0, 0), (1, 0), (2, 0), (3, 0)
O0, O1, O2, O3 = (0, 1), (1, 1), (2, 1), (3, 1)
PLACES = (S0, S1, S2, S3, O0, O1, O2, O3)
f32, bf16 = jnp.float32, jnp.bfloat16


def split_index(axis, index):
    return (index // PAIR, index % PAIR) if axis == "row" else (index % RING, index // RING)


def join_index(axis, ring, pair):
    return ring * PAIR + pair if axis == "row" else pair * RING + ring


def pairs(axes, move):
    out = []
    for row in range(8):
        for col in range(8):
            for mat in range(2):
                axis = axes[mat]
                if axis is None:
                    continue
                ring, pair = split_index(axis, row if axis == "row" else col)
                ring, pair = ((ring + move) % RING, pair) if move else (ring, 1 - pair)
                there = join_index(axis, ring, pair)
                to = (there, col) if axis == "row" else (row, there)
                out.append(((row * 8 + col) * 2 + mat, (to[0] * 8 + to[1]) * 2 + mat))
    return out


def send(value, axes, move):
    return lax.ppermute(value, AXES, pairs(axes, move))


def member(axes, place):
    found = []
    for axis in axes:
        ring, pair = split_index(axis, lax.axis_index(axis))
        found.append(join_index(axis, (ring + place[0]) % RING, (pair + place[1]) % PAIR))
    return jnp.where(lax.axis_index("mat") == 0, found[0], found[1]).astype(jnp.int32)


def chunks(n):
    return [slice(i, min(i + 256, n)) for i in range(0, n, 256)]


def stay(x):
    return pltpu.with_memory_space_constraint(x, pltpu.VMEM)


def leave_out(x):
    return pltpu.with_memory_space_constraint(x, pltpu.HBM)


def kept_array(x):
    return pltpu.VMEM(x.shape, x.dtype)


def call(body, outs, *args, flops=0, scratch=(), after=(), leave=0, loose=0):
    vmem, place = pl.BlockSpec(memory_space=pltpu.VMEM), pl.BlockSpec(memory_space=pl.ANY)
    inputs = len(args)
    held = sum(x.size * x.dtype.itemsize for x in (*args[1:], *outs[:leave], *scratch) if x.ndim == 2)

    def whole(*refs):
        body(*refs[:inputs], *refs[inputs + len(after) :])

    return pl.pallas_call(
        whole,
        out_shape=[x if i < leave else kept_array(x) for i, x in enumerate(outs)],
        in_specs=[pl.BlockSpec(memory_space=pltpu.SMEM)] + [vmem] * (inputs - 1) + [place] * len(after),
        out_specs=[vmem] * len(outs),
        scratch_shapes=[pltpu.VMEM(x.shape, x.dtype) for x in scratch],
        compiler_params=pltpu.CompilerParams(vmem_limit_bytes=held + 4 * 2**20),
        cost_estimate=pl.CostEstimate(flops=flops, bytes_accessed=0, transcendentals=0),
    )(args[0], *[x if i < loose else stay(x) for i, x in enumerate(args[1:])], *after)


def block_of(scalars, place):
    return scalars[1 + PLACES.index(place)]


def write_term(own, w, index, out):
    for n in chunks(out.shape[1]):
        out[:, n] = jnp.dot(own[...], w[index, :, n], preferred_element_type=f32).astype(bf16)


def weighed(s, w, pairs, n):
    parts = [jnp.dot(w[block_of(s, p)], x[:, n], preferred_element_type=f32) for p, x in pairs]
    while len(parts) > 1:
        parts = [a + b for a, b in zip(parts[0::2], parts[1::2], strict=True)]
    return parts[0]


def write_first(s, w, own, u, d):
    @pl.when(s[0] == 1)
    def _():
        u[...] = own[...]
        d[...] = own[...]

    @pl.when(s[0] == 0)
    def _():
        write_term(own, w, block_of(s, O2), u)
        write_term(own, w, block_of(s, S2), d)


def both(axes, gathers, scalars, weights, own, first, finish, extra, outs, leave=0, following=None, early=(), late=()):
    one = tuple(a if m == gathers else None for m, a in enumerate(axes))
    other = tuple(a if m != gathers else None for m, a in enumerate(axes))
    n = own.shape[1]
    block = jax.ShapeDtypeStruct(own.shape, bf16)
    acc = jax.ShapeDtypeStruct((n, n), f32)
    cost = 2 * n**3
    u, d = first
    across, up, down = send(own, one, 0), send(u, axes, 1), send(d, axes, -1)

    kept = (O1, O3, O0, S1, S3, S0)

    def terms_body(s, w, a, *out):
        @pl.when(s[0] == 0)
        def _():
            for place, o in zip(kept, out, strict=True):
                write_term(a, w, block_of(s, place), o)

    term = dict(zip(kept, call(terms_body, [block] * 6, scalars, weights, own, flops=6 * cost), strict=True))

    def down1_body(s, c, p3, od):
        @pl.when(s[0] == 1)
        def _():
            od[...] = c[...]

        @pl.when(s[0] == 0)
        def _():
            od[...] = p3[...]

    def up1_body(s, c, u, p1, ou):
        @pl.when(s[0] == 1)
        def _():
            ou[...] = c[...]

        @pl.when(s[0] == 0)
        def _():
            ou[...] = (p1[...].astype(f32) + u[...].astype(f32)).astype(bf16)

    (d,) = call(down1_body, [block], scalars, across, term[O3])
    down1 = send(d, axes, -1)
    (u,) = call(up1_body, [block], scalars, across, up, term[O1], after=early)
    up1 = send(u, axes, 1)

    def weigh1_body(s, w, o, u, d, c, out):
        @pl.when(s[0] == 1)
        def _():
            for k in chunks(n):
                out[:, k] = weighed(s, w, ((S0, o), (S3, u), (S1, d), (O0, c)), k)

    total = call(weigh1_body, [acc], scalars, weights, own, up, down, across, flops=4 * cost)[0]

    def over_body(s, u1, d1, p0, oo):
        @pl.when(s[0] == 0)
        def _():
            oo[...] = (p0[...].astype(f32) + u1[...].astype(f32) + d1[...].astype(f32)).astype(bf16)

    def up2_body(s, u, q1, ou):
        @pl.when(s[0] == 1)
        def _():
            ou[...] = u[...]

        @pl.when(s[0] == 0)
        def _():
            ou[...] = q1[...]

    def down2_body(s, d, d1, q3, od):
        @pl.when(s[0] == 1)
        def _():
            od[...] = d1[...]

        @pl.when(s[0] == 0)
        def _():
            od[...] = (q3[...].astype(f32) + d[...].astype(f32)).astype(bf16)

    (u,) = call(up2_body, [block], scalars, up, term[S1])
    (o,) = call(over_body, [block], scalars, up1, down1, term[O0], after=(total, u, *late))
    (d,) = call(down2_body, [block], scalars, down, down1, term[S3], after=(o,))
    over, up2, down2 = send(o, other, 0), send(u, axes, 1), send(d, axes, -1)

    def weigh2_body(s, w, t, u, d, p, c, out):
        @pl.when(s[0] == 1)
        def _():
            for k in chunks(n):
                out[:, k] = t[:, k] + weighed(s, w, ((O3, u), (O1, d)), k)

        @pl.when(s[0] == 0)
        def _():
            out[...] = p[...].astype(f32) + c[...].astype(f32)

    total = call(weigh2_body, [acc], scalars, weights, total, up1, down1, term[S0], over, flops=2 * cost)[0]
    ahead = [] if following is None else following
    opened = [block] * len(ahead)

    def last_body(s, w, t, u, d, *refs):
        then, refs = refs[: len(ahead)], refs[len(ahead) :]
        more, refs = refs[: len(extra)], refs[len(extra) :]
        out, begin, scratch = refs[: len(outs)], refs[len(outs) : -1], refs[-1]

        @pl.when(s[0] == 1)
        def _():
            for k in chunks(n):
                scratch[:, k] = t[:, k] + weighed(s, w, ((S2, u), (O2, d)), k)

        @pl.when(s[0] == 0)
        def _():
            scratch[...] = t[...] + (u[...].astype(f32) + d[...].astype(f32))

        finish(scratch, more, out)
        if ahead:
            write_first(*then, out[-1], *begin)

    return call(
        last_body, [*outs, *opened], scalars, weights, total, up2, down2, *ahead, *extra,
        flops=2 * cost, scratch=[acc], leave=leave,
    )


def stacked(scalars, blocks, after=(), far=False):
    flat = [x for block in blocks for x in (block if isinstance(block, tuple) else (block,))]
    n = flat[0].shape[1]

    def body(s, *refs):
        out, sems, copies, at = refs[-2], refs[-1], [], 0
        for place, block in zip(PLACES, blocks, strict=True):
            row = 0
            for x in block if isinstance(block, tuple) else (block,):
                target = out.at[block_of(s, place), pl.ds(row, x.shape[0])]
                copies.append(pltpu.make_async_copy(refs[at], target, sems.at[at]))
                row += x.shape[0]
                at += 1
        for copy in copies:
            copy.start()
        for copy in copies:
            copy.wait()

    place = pl.BlockSpec(memory_space=pl.ANY)
    return pl.pallas_call(
        lambda s, *refs: body(s, *refs[: len(flat)], *refs[len(flat) + len(after) :]),
        out_shape=kept_array(jax.ShapeDtypeStruct((8, n, n), bf16)),
        in_specs=[pl.BlockSpec(memory_space=pltpu.SMEM)] + [place] * (len(flat) + len(after)),
        out_specs=pl.BlockSpec(memory_space=pltpu.VMEM),
        scratch_shapes=[pltpu.SemaphoreType.DMA((len(flat),))],
        compiler_params=pltpu.CompilerParams(vmem_limit_bytes=4 * 2**20),
        cost_estimate=pl.CostEstimate(flops=0, bytes_accessed=2 * 8 * n * n * 2, transcendentals=0),
    )(scalars, *[leave_out(x) if far else x for x in flat], *after)


def tied(value, after=()):
    place = pl.BlockSpec(memory_space=pl.ANY)
    return pl.pallas_call(
        lambda *refs: None,
        out_shape=jax.ShapeDtypeStruct(value.shape, value.dtype),
        in_specs=[place] * (1 + len(after)),
        out_specs=place,
        input_output_aliases={0: 0},
        cost_estimate=pl.CostEstimate(flops=0, bytes_accessed=0, transcendentals=0),
    )(value, *after)


def copied(scalars, value, after):
    def body(s, x, o):
        o[...] = x[...]

    return call(body, [jax.ShapeDtypeStruct(value.shape, value.dtype)], scalars, value, after=after)[0]


def to_block(total, more, out):
    out[0][...] = total[...].astype(bf16)


def moments(total, more, out):
    n = total.shape[0]
    for k in [slice(i, i + n // 5) for i in range(0, n, n // 5)]:
        rotated = total[:, k]
        first = beta_value * more[0][:, k] + (1.0 - beta_value) * rotated
        second = beta_value * more[1][:, k] + (1.0 - beta_value) * rotated * rotated
        out[0][:, k] = first
        out[1][:, k] = second
        quotient = first / bias_fix / (jnp.sqrt(second / bias_fix) + eps_value)
        out[2][k, :] = quotient.astype(bf16).T


def turned(total, more, out):
    out[0][...] = total[...].astype(bf16).T


def placed_bases(mat, left, right):
    n = left.shape[0]
    block = jax.ShapeDtypeStruct((n, n), bf16)

    def body(s, left, right, one, two, x, y, sems):
        copies = [pltpu.make_async_copy(left, x, sems.at[0]), pltpu.make_async_copy(right, y, sems.at[1])]
        for copy in copies:
            copy.start()
        for copy in copies:
            copy.wait()

        @pl.when(s[0] == 0)
        def _():
            one[...] = x[...].T
            two[...] = y[...]

        @pl.when(s[0] == 1)
        def _():
            one[...] = y[...]
            two[...] = x[...].T

    place, vmem = pl.BlockSpec(memory_space=pl.ANY), pl.BlockSpec(memory_space=pltpu.VMEM)
    return pl.pallas_call(
        body,
        out_shape=[kept_array(block)] * 2,
        in_specs=[pl.BlockSpec(memory_space=pltpu.SMEM), place, place],
        out_specs=[vmem] * 2,
        scratch_shapes=[pltpu.VMEM((n, n), bf16), pltpu.VMEM((n, n), bf16), pltpu.SemaphoreType.DMA((2,))],
        compiler_params=pltpu.CompilerParams(vmem_limit_bytes=8 * 2**20),
        cost_estimate=pl.CostEstimate(flops=0, bytes_accessed=4 * n * n * 2, transcendentals=0),
    )(mat, leave_out(left), leave_out(right))


def shards(gradient, left_basis, right_basis, first_moment, second_moment):
    grad, left, right = gradient[0], left_basis[0], right_basis[0]
    mat = lax.axis_index("mat").astype(jnp.int32)
    a, b = ("col", "row"), ("row", "col")

    def scalars(gathers, axes):
        return jnp.stack([mat if gathers else 1 - mat] + [member(axes, p) for p in PLACES])

    slot2, slot4, slot5, slot6 = scalars(0, b), scalars(1, a), scalars(0, a), scalars(1, b)
    n = grad.shape[0]
    block, whole = jax.ShapeDtypeStruct((n, n), bf16), jax.ShapeDtypeStruct((n, n), f32)
    one, two = placed_bases(mat[None], left, right)

    across, up, down = send(one, a, 0), send(one, a, 1), send(one, a, -1)
    upb, downb = send(two, b, 1), send(two, b, -1)
    relay = tied(across, (up, down, upb, downb))
    up1, down1, up2 = send(relay, a, 1), send(relay, a, -1), send(up, a, 1)
    acrossb = send(copied(slot2, two, (relay,)), b, 0)
    down2 = send(down1, a, -1)
    gathered_a = (one, down, up2, up, relay, down1, down2, up1)
    weights_a = stacked(slot5, gathered_a)

    first = call(write_first, [block] * 2, slot2, weights_a, grad, flops=4 * n**3)
    upb1, downb1 = send(acrossb, b, 1), send(acrossb, b, -1)
    upb2 = send(upb, b, 1)
    downb2 = send(downb1, b, -1)
    weights_b = stacked(slot2, (two, downb, upb2, upb, acrossb, downb1, downb2, upb1))
    middle, *first = both(
        b, 0, slot2, weights_a, grad, first, to_block, (), [block], 0, (slot4, weights_b), (),
        (upb2, downb1),
    )
    new_first, new_second, normalized, *first = both(
        a, 1, slot4, weights_b, middle, first, moments, (first_moment[0], second_moment[0]), [whole, whole, block],
        2, (slot5, weights_b),
    )
    weights_a = stacked(slot5, gathered_a, (normalized,), True)
    middle, *first = both(
        a, 0, slot5, weights_b, normalized, first, to_block, (), [block], 0, (slot6, weights_a), (), (weights_a,)
    )
    (update,) = both(b, 1, slot6, weights_a, middle, first, turned, (), [block], 1)
    return update[None], new_first[None], new_second[None]


def solution(mesh):
    placed = (
        P("mat", "row", "col"),
        P("mat", "col", "row"),
        P("mat", "col", "row"),
        P("mat", "row", "col"),
        P("mat", "row", "col"),
    )
    return jax.shard_map(
        shards,
        mesh=mesh,
        in_specs=placed,
        out_specs=(P("mat", "row", "col"), P("mat", "row", "col"), P("mat", "row", "col")),
        check_vma=False,
    )
```

```python
import functools
import jax
import jax.numpy as jnp
from jax import lax
from jax.experimental import pallas as pl
from jax.experimental.pallas import tpu as pltpu
from jax.sharding import PartitionSpec as P

beta_value = 0.95
bias_fix = 1.0 - 0.95**10
eps_value = 1e-08

AXES = ("row", "col", "mat")
RING, PAIR = 4, 2
S0, S1, S2, S3 = (0, 0), (1, 0), (2, 0), (3, 0)
O0, O1, O2, O3 = (0, 1), (1, 1), (2, 1), (3, 1)
PLACES = (S0, S1, S2, S3, O0, O1, O2, O3)
f32, bf16 = jnp.float32, jnp.bfloat16


def split_index(axis, index):
    return (index // PAIR, index % PAIR) if axis == "row" else (index % RING, index // RING)


def join_index(axis, ring, pair):
    return ring * PAIR + pair if axis == "row" else pair * RING + ring


def pairs(axes, move):
    out = []
    for row in range(8):
        for col in range(8):
            for mat in range(2):
                axis = axes[mat]
                if axis is None:
                    continue
                ring, pair = split_index(axis, row if axis == "row" else col)
                ring, pair = ((ring + move) % RING, pair) if move else (ring, 1 - pair)
                there = join_index(axis, ring, pair)
                to = (there, col) if axis == "row" else (row, there)
                out.append(((row * 8 + col) * 2 + mat, (to[0] * 8 + to[1]) * 2 + mat))
    return out


def send(value, axes, move):
    return lax.ppermute(value, AXES, pairs(axes, move))


def member(axes, place):
    found = []
    for axis in axes:
        ring, pair = split_index(axis, lax.axis_index(axis))
        found.append(join_index(axis, (ring + place[0]) % RING, (pair + place[1]) % PAIR))
    return jnp.where(lax.axis_index("mat") == 0, found[0], found[1]).astype(jnp.int32)


def chunks(n):
    return [slice(i, min(i + 256, n)) for i in range(0, n, 256)]


def stay(x):
    return pltpu.with_memory_space_constraint(x, pltpu.VMEM)


def leave_out(x):
    return pltpu.with_memory_space_constraint(x, pltpu.HBM)


def kept_array(x):
    return pltpu.VMEM(x.shape, x.dtype)


def call(body, outs, *args, flops=0, scratch=(), after=(), leave=0, loose=0):
    vmem, place = pl.BlockSpec(memory_space=pltpu.VMEM), pl.BlockSpec(memory_space=pl.ANY)
    inputs = len(args)
    held = sum(x.size * x.dtype.itemsize for x in (*args[1:], *outs[:leave], *scratch) if x.ndim == 2)

    def whole(*refs):
        body(*refs[:inputs], *refs[inputs + len(after) :])

    return pl.pallas_call(
        whole,
        out_shape=[x if i < leave else kept_array(x) for i, x in enumerate(outs)],
        in_specs=[pl.BlockSpec(memory_space=pltpu.SMEM)] + [vmem] * (inputs - 1) + [place] * len(after),
        out_specs=[vmem] * len(outs),
        scratch_shapes=[pltpu.VMEM(x.shape, x.dtype) for x in scratch],
        compiler_params=pltpu.CompilerParams(vmem_limit_bytes=held + 4 * 2**20),
        cost_estimate=pl.CostEstimate(flops=flops, bytes_accessed=0, transcendentals=0),
    )(args[0], *[x if i < loose else stay(x) for i, x in enumerate(args[1:])], *after)


def block_of(scalars, place):
    return scalars[1 + PLACES.index(place)]


def write_term(own, w, index, out):
    for n in chunks(out.shape[1]):
        out[:, n] = jnp.dot(own[...], w[index, :, n], preferred_element_type=f32).astype(bf16)


def weighed(s, w, pairs, n):
    parts = [jnp.dot(w[block_of(s, p)], x[:, n], preferred_element_type=f32) for p, x in pairs]
    while len(parts) > 1:
        parts = [a + b for a, b in zip(parts[0::2], parts[1::2], strict=True)]
    return parts[0]


def write_first(s, w, own, u, d):
    @pl.when(s[0] == 1)
    def _():
        u[...] = own[...]
        d[...] = own[...]

    @pl.when(s[0] == 0)
    def _():
        write_term(own, w, block_of(s, O2), u)
        write_term(own, w, block_of(s, S2), d)


def both(axes, gathers, scalars, weights, own, first, finish, extra, outs, leave=0, following=None, early=(), late=()):
    one = tuple(a if m == gathers else None for m, a in enumerate(axes))
    other = tuple(a if m != gathers else None for m, a in enumerate(axes))
    n = own.shape[1]
    block = jax.ShapeDtypeStruct(own.shape, bf16)
    acc = jax.ShapeDtypeStruct((n, n), f32)
    cost = 2 * n**3
    u, d = first
    across, up, down = send(own, one, 0), send(u, axes, 1), send(d, axes, -1)

    kept = (O1, O3, O0, S1, S3, S0)

    def terms_body(s, w, a, *out):
        @pl.when(s[0] == 0)
        def _():
            for place, o in zip(kept, out, strict=True):
                write_term(a, w, block_of(s, place), o)

    term = dict(zip(kept, call(terms_body, [block] * 6, scalars, weights, own, flops=6 * cost), strict=True))

    def step1_body(s, c, u, p1, p3, q1, ou, od, ou2):
        @pl.when(s[0] == 1)
        def _():
            ou[...] = c[...]
            od[...] = c[...]
            ou2[...] = u[...]

        @pl.when(s[0] == 0)
        def _():
            ou[...] = (p1[...].astype(f32) + u[...].astype(f32)).astype(bf16)
            od[...] = p3[...]
            ou2[...] = q1[...]

    u, d, third = call(
        step1_body, [block] * 3, scalars, across, up, term[O1], term[O3], term[S1], after=early
    )
    up1, down1 = send(u, axes, 1), send(d, axes, -1)

    def weigh1_body(s, w, o, u, d, c, out):
        @pl.when(s[0] == 1)
        def _():
            for k in chunks(n):
                out[:, k] = weighed(s, w, ((S0, o), (S3, u), (S1, d), (O0, c)), k)

    total = call(weigh1_body, [acc], scalars, weights, own, up, down, across, flops=4 * cost)[0]

    def step2_body(s, d, u1, d1, p0, q3, oo, od):
        @pl.when(s[0] == 1)
        def _():
            od[...] = d1[...]

        @pl.when(s[0] == 0)
        def _():
            oo[...] = (p0[...].astype(f32) + u1[...].astype(f32) + d1[...].astype(f32)).astype(bf16)
            od[...] = (q3[...].astype(f32) + d[...].astype(f32)).astype(bf16)

    o, d = call(
        step2_body, [block] * 2, scalars, down, up1, down1, term[O0], term[S3], after=(total, *late)
    )
    over, up2, down2 = send(o, other, 0), send(third, axes, 1), send(d, axes, -1)

    def weigh2_body(s, w, t, u, d, p, c, out):
        @pl.when(s[0] == 1)
        def _():
            for k in chunks(n):
                out[:, k] = t[:, k] + weighed(s, w, ((O3, u), (O1, d)), k)

        @pl.when(s[0] == 0)
        def _():
            out[...] = p[...].astype(f32) + c[...].astype(f32)

    total = call(weigh2_body, [acc], scalars, weights, total, up1, down1, term[S0], over, flops=2 * cost)[0]
    ahead = [] if following is None else following
    opened = [block] * len(ahead)

    def last_body(s, w, t, u, d, *refs):
        then, refs = refs[: len(ahead)], refs[len(ahead) :]
        more, refs = refs[: len(extra)], refs[len(extra) :]
        out, begin, scratch = refs[: len(outs)], refs[len(outs) : -1], refs[-1]

        @pl.when(s[0] == 1)
        def _():
            for k in chunks(n):
                scratch[:, k] = t[:, k] + weighed(s, w, ((S2, u), (O2, d)), k)

        @pl.when(s[0] == 0)
        def _():
            scratch[...] = t[...] + (u[...].astype(f32) + d[...].astype(f32))

        finish(scratch, more, out)
        if ahead:
            write_first(*then, out[-1], *begin)

    return call(
        last_body, [*outs, *opened], scalars, weights, total, up2, down2, *ahead, *extra,
        flops=2 * cost, scratch=[acc], leave=leave,
    )


def stacked(scalars, blocks, after=(), far=False):
    flat = [x for block in blocks for x in (block if isinstance(block, tuple) else (block,))]
    n = flat[0].shape[1]

    def body(s, *refs):
        out, sems, copies, at = refs[-2], refs[-1], [], 0
        for place, block in zip(PLACES, blocks, strict=True):
            row = 0
            for x in block if isinstance(block, tuple) else (block,):
                target = out.at[block_of(s, place), pl.ds(row, x.shape[0])]
                copies.append(pltpu.make_async_copy(refs[at], target, sems.at[at]))
                row += x.shape[0]
                at += 1
        for copy in copies:
            copy.start()
        for copy in copies:
            copy.wait()

    place = pl.BlockSpec(memory_space=pl.ANY)
    return pl.pallas_call(
        lambda s, *refs: body(s, *refs[: len(flat)], *refs[len(flat) + len(after) :]),
        out_shape=kept_array(jax.ShapeDtypeStruct((8, n, n), bf16)),
        in_specs=[pl.BlockSpec(memory_space=pltpu.SMEM)] + [place] * (len(flat) + len(after)),
        out_specs=pl.BlockSpec(memory_space=pltpu.VMEM),
        scratch_shapes=[pltpu.SemaphoreType.DMA((len(flat),))],
        compiler_params=pltpu.CompilerParams(vmem_limit_bytes=4 * 2**20),
        cost_estimate=pl.CostEstimate(flops=0, bytes_accessed=2 * 8 * n * n * 2, transcendentals=0),
    )(scalars, *[leave_out(x) if far else x for x in flat], *after)


def tied(value, after=()):
    place = pl.BlockSpec(memory_space=pl.ANY)
    return pl.pallas_call(
        lambda *refs: None,
        out_shape=jax.ShapeDtypeStruct(value.shape, value.dtype),
        in_specs=[place] * (1 + len(after)),
        out_specs=place,
        input_output_aliases={0: 0},
        cost_estimate=pl.CostEstimate(flops=0, bytes_accessed=0, transcendentals=0),
    )(value, *after)


def to_block(total, more, out):
    out[0][...] = total[...].astype(bf16)


def moments(total, more, out):
    n = total.shape[0]
    for k in [slice(i, i + n // 5) for i in range(0, n, n // 5)]:
        rotated = total[:, k]
        first = beta_value * more[0][:, k] + (1.0 - beta_value) * rotated
        second = beta_value * more[1][:, k] + (1.0 - beta_value) * rotated * rotated
        out[0][:, k] = first
        out[1][:, k] = second
        quotient = first / bias_fix / (jnp.sqrt(second / bias_fix) + eps_value)
        out[2][k, :] = quotient.astype(bf16).T


def turned(total, more, out):
    out[0][...] = total[...].astype(bf16).T


def placed_bases(mat, left, right):
    n = left.shape[0]
    block = jax.ShapeDtypeStruct((n, n), bf16)

    def body(s, left, right, one, two, x, y, sems):
        copies = [pltpu.make_async_copy(left, x, sems.at[0]), pltpu.make_async_copy(right, y, sems.at[1])]
        for copy in copies:
            copy.start()
        for copy in copies:
            copy.wait()

        @pl.when(s[0] == 0)
        def _():
            one[...] = x[...].T
            two[...] = y[...]

        @pl.when(s[0] == 1)
        def _():
            one[...] = y[...]
            two[...] = x[...].T

    place, vmem = pl.BlockSpec(memory_space=pl.ANY), pl.BlockSpec(memory_space=pltpu.VMEM)
    return pl.pallas_call(
        body,
        out_shape=[kept_array(block)] * 2,
        in_specs=[pl.BlockSpec(memory_space=pltpu.SMEM), place, place],
        out_specs=[vmem] * 2,
        scratch_shapes=[pltpu.VMEM((n, n), bf16), pltpu.VMEM((n, n), bf16), pltpu.SemaphoreType.DMA((2,))],
        compiler_params=pltpu.CompilerParams(vmem_limit_bytes=8 * 2**20),
        cost_estimate=pl.CostEstimate(flops=0, bytes_accessed=4 * n * n * 2, transcendentals=0),
    )(mat, leave_out(left), leave_out(right))


def shards(gradient, left_basis, right_basis, first_moment, second_moment):
    grad, left, right = gradient[0], left_basis[0], right_basis[0]
    mat = lax.axis_index("mat").astype(jnp.int32)
    a, b = ("col", "row"), ("row", "col")

    def scalars(gathers, axes):
        return jnp.stack([mat if gathers else 1 - mat] + [member(axes, p) for p in PLACES])

    slot2, slot4, slot5, slot6 = scalars(0, b), scalars(1, a), scalars(0, a), scalars(1, b)
    n = grad.shape[0]
    block, whole = jax.ShapeDtypeStruct((n, n), bf16), jax.ShapeDtypeStruct((n, n), f32)
    one, two = placed_bases(mat[None], left, right)

    across, up, down = send(one, a, 0), send(one, a, 1), send(one, a, -1)
    upb, downb = send(two, b, 1), send(two, b, -1)
    relay = tied(across, (up, down, upb, downb))
    up1, down1, up2 = send(relay, a, 1), send(relay, a, -1), send(up, a, 1)
    two = tied(two, (relay,))
    acrossb = send(two, b, 0)
    down2 = send(down1, a, -1)
    gathered_a = (one, down, up2, up, relay, down1, down2, up1)
    weights_a = stacked(slot5, gathered_a)

    first = call(write_first, [block] * 2, slot2, weights_a, grad, flops=4 * n**3)
    upb1, downb1 = send(acrossb, b, 1), send(acrossb, b, -1)
    upb2 = send(upb, b, 1)
    downb2 = send(downb1, b, -1)
    weights_b = stacked(slot2, (two, downb, upb2, upb, acrossb, downb1, downb2, upb1))
    middle, *first = both(
        b, 0, slot2, weights_a, grad, first, to_block, (), [block], 0, (slot4, weights_b), (),
        (upb2, downb1),
    )
    new_first, new_second, normalized, *first = both(
        a, 1, slot4, weights_b, middle, first, moments, (first_moment[0], second_moment[0]), [whole, whole, block],
        2, (slot5, weights_b),
    )
    weights_a = stacked(slot5, gathered_a, (normalized,), True)
    middle, *first = both(
        a, 0, slot5, weights_b, normalized, first, to_block, (), [block], 0, (slot6, weights_a), (), (weights_a,)
    )
    (update,) = both(b, 1, slot6, weights_a, middle, first, turned, (), [block], 1)
    return update[None], new_first[None], new_second[None]


def solution(mesh):
    placed = (
        P("mat", "row", "col"),
        P("mat", "col", "row"),
        P("mat", "col", "row"),
        P("mat", "row", "col"),
        P("mat", "row", "col"),
    )
    return jax.shard_map(
        shards,
        mesh=mesh,
        in_specs=placed,
        out_specs=(P("mat", "row", "col"), P("mat", "row", "col"), P("mat", "row", "col")),
        check_vma=False,
    )
```

```python
import functools
import jax
import jax.numpy as jnp
from jax import lax
from jax.experimental import pallas as pl
from jax.experimental.pallas import tpu as pltpu
from jax.sharding import PartitionSpec as P

beta_value = 0.95
bias_fix = 1.0 - 0.95**10
eps_value = 1e-08

AXES = ("row", "col", "mat")
RING, PAIR = 4, 2
S0, S1, S2, S3 = (0, 0), (1, 0), (2, 0), (3, 0)
O0, O1, O2, O3 = (0, 1), (1, 1), (2, 1), (3, 1)
PLACES = (S0, S1, S2, S3, O0, O1, O2, O3)
f32, bf16 = jnp.float32, jnp.bfloat16


def split_index(axis, index):
    return (index // PAIR, index % PAIR) if axis == "row" else (index % RING, index // RING)


def join_index(axis, ring, pair):
    return ring * PAIR + pair if axis == "row" else pair * RING + ring


def pairs(axes, move):
    out = []
    for row in range(8):
        for col in range(8):
            for mat in range(2):
                axis = axes[mat]
                if axis is None:
                    continue
                ring, pair = split_index(axis, row if axis == "row" else col)
                ring, pair = ((ring + move) % RING, pair) if move else (ring, 1 - pair)
                there = join_index(axis, ring, pair)
                to = (there, col) if axis == "row" else (row, there)
                out.append(((row * 8 + col) * 2 + mat, (to[0] * 8 + to[1]) * 2 + mat))
    return out


def send(value, axes, move):
    return lax.ppermute(value, AXES, pairs(axes, move))


def member(axes, place):
    found = []
    for axis in axes:
        ring, pair = split_index(axis, lax.axis_index(axis))
        found.append(join_index(axis, (ring + place[0]) % RING, (pair + place[1]) % PAIR))
    return jnp.where(lax.axis_index("mat") == 0, found[0], found[1]).astype(jnp.int32)


def chunks(n):
    return [slice(i, min(i + 256, n)) for i in range(0, n, 256)]


def stay(x):
    return pltpu.with_memory_space_constraint(x, pltpu.VMEM)


def leave_out(x):
    return pltpu.with_memory_space_constraint(x, pltpu.HBM)


def kept_array(x):
    return pltpu.VMEM(x.shape, x.dtype)


def call(body, outs, *args, flops=0, scratch=(), after=(), leave=0, loose=0):
    vmem, place = pl.BlockSpec(memory_space=pltpu.VMEM), pl.BlockSpec(memory_space=pl.ANY)
    inputs = len(args)
    held = sum(x.size * x.dtype.itemsize for x in (*args[1:], *outs[:leave], *scratch) if x.ndim == 2)

    def whole(*refs):
        body(*refs[:inputs], *refs[inputs + len(after) :])

    return pl.pallas_call(
        whole,
        out_shape=[x if i < leave else kept_array(x) for i, x in enumerate(outs)],
        in_specs=[pl.BlockSpec(memory_space=pltpu.SMEM)] + [vmem] * (inputs - 1) + [place] * len(after),
        out_specs=[vmem] * len(outs),
        scratch_shapes=[pltpu.VMEM(x.shape, x.dtype) for x in scratch],
        compiler_params=pltpu.CompilerParams(vmem_limit_bytes=held + 4 * 2**20),
        cost_estimate=pl.CostEstimate(flops=flops, bytes_accessed=0, transcendentals=0),
    )(args[0], *[x if i < loose else stay(x) for i, x in enumerate(args[1:])], *after)


def block_of(scalars, place):
    return scalars[1 + PLACES.index(place)]


def write_term(own, w, index, out):
    for n in chunks(out.shape[1]):
        out[:, n] = jnp.dot(own[...], w[index, :, n], preferred_element_type=f32).astype(bf16)


def weighed(s, w, pairs, n):
    parts = [jnp.dot(w[block_of(s, p)], x[:, n], preferred_element_type=f32) for p, x in pairs]
    while len(parts) > 1:
        parts = [a + b for a, b in zip(parts[0::2], parts[1::2], strict=True)]
    return parts[0]


def write_first(s, w, own, u, d):
    @pl.when(s[0] == 1)
    def _():
        u[...] = own[...]
        d[...] = own[...]

    @pl.when(s[0] == 0)
    def _():
        write_term(own, w, block_of(s, O2), u)
        write_term(own, w, block_of(s, S2), d)


def both(axes, gathers, scalars, weights, own, first, finish, extra, outs, leave=0, following=None, early=(), late=()):
    one = tuple(a if m == gathers else None for m, a in enumerate(axes))
    other = tuple(a if m != gathers else None for m, a in enumerate(axes))
    n = own.shape[1]
    block = jax.ShapeDtypeStruct(own.shape, bf16)
    acc = jax.ShapeDtypeStruct((n, n), f32)
    cost = 2 * n**3
    u, d = first
    across, up, down = send(own, one, 0), send(u, axes, 1), send(d, axes, -1)

    kept = (O1, O3, O0, S1, S3, S0)

    def terms_body(s, w, a, *out):
        @pl.when(s[0] == 0)
        def _():
            for place, o in zip(kept, out, strict=True):
                write_term(a, w, block_of(s, place), o)

    term = dict(zip(kept, call(terms_body, [block] * 6, scalars, weights, own, flops=6 * cost), strict=True))

    def step1_body(s, c, u, p1, p3, q1, ou, od, ou2):
        @pl.when(s[0] == 1)
        def _():
            ou[...] = c[...]
            od[...] = c[...]
            ou2[...] = u[...]

        @pl.when(s[0] == 0)
        def _():
            ou[...] = (p1[...].astype(f32) + u[...].astype(f32)).astype(bf16)
            od[...] = p3[...]
            ou2[...] = q1[...]

    u, d, third = call(
        step1_body, [block] * 3, scalars, across, up, term[O1], term[O3], term[S1], after=early
    )
    up1, down1 = send(u, axes, 1), send(d, axes, -1)

    def weigh1_body(s, w, o, u, d, c, out):
        @pl.when(s[0] == 1)
        def _():
            for k in chunks(n):
                out[:, k] = weighed(s, w, ((S0, o), (S3, u), (S1, d), (O0, c)), k)

    total = call(weigh1_body, [acc], scalars, weights, own, up, down, across, flops=4 * cost)[0]

    def step2_body(s, d, u1, d1, p0, q3, oo, od):
        @pl.when(s[0] == 1)
        def _():
            od[...] = d1[...]

        @pl.when(s[0] == 0)
        def _():
            oo[...] = (p0[...].astype(f32) + u1[...].astype(f32) + d1[...].astype(f32)).astype(bf16)
            od[...] = (q3[...].astype(f32) + d[...].astype(f32)).astype(bf16)

    o, d = call(
        step2_body, [block] * 2, scalars, down, up1, down1, term[O0], term[S3], after=(total, *late)
    )
    over, up2, down2 = send(o, other, 0), send(third, axes, 1), send(d, axes, -1)

    def weigh2_body(s, w, t, u, d, p, c, out):
        @pl.when(s[0] == 1)
        def _():
            for k in chunks(n):
                out[:, k] = t[:, k] + weighed(s, w, ((O3, u), (O1, d)), k)

        @pl.when(s[0] == 0)
        def _():
            out[...] = p[...].astype(f32) + c[...].astype(f32)

    total = call(weigh2_body, [acc], scalars, weights, total, up1, down1, term[S0], over, flops=2 * cost)[0]
    ahead = [] if following is None else following
    opened = [block] * len(ahead)

    def last_body(s, w, t, u, d, *refs):
        then, refs = refs[: len(ahead)], refs[len(ahead) :]
        more, refs = refs[: len(extra)], refs[len(extra) :]
        out, begin, scratch = refs[: len(outs)], refs[len(outs) : -1], refs[-1]

        @pl.when(s[0] == 1)
        def _():
            for k in chunks(n):
                scratch[:, k] = t[:, k] + weighed(s, w, ((S2, u), (O2, d)), k)

        @pl.when(s[0] == 0)
        def _():
            scratch[...] = t[...] + (u[...].astype(f32) + d[...].astype(f32))

        finish(scratch, more, out)
        if ahead:
            write_first(*then, out[-1], *begin)

    return call(
        last_body, [*outs, *opened], scalars, weights, total, up2, down2, *ahead, *extra,
        flops=2 * cost, scratch=[acc], leave=leave,
    )


def stacked(scalars, blocks, after=(), far=False):
    flat = [x for block in blocks for x in (block if isinstance(block, tuple) else (block,))]
    n = flat[0].shape[1]

    def body(s, *refs):
        out, sems, copies, at = refs[-2], refs[-1], [], 0
        for place, block in zip(PLACES, blocks, strict=True):
            row = 0
            for x in block if isinstance(block, tuple) else (block,):
                target = out.at[block_of(s, place), pl.ds(row, x.shape[0])]
                copies.append(pltpu.make_async_copy(refs[at], target, sems.at[at]))
                row += x.shape[0]
                at += 1
        for copy in copies:
            copy.start()
        for copy in copies:
            copy.wait()

    place = pl.BlockSpec(memory_space=pl.ANY)
    return pl.pallas_call(
        lambda s, *refs: body(s, *refs[: len(flat)], *refs[len(flat) + len(after) :]),
        out_shape=kept_array(jax.ShapeDtypeStruct((8, n, n), bf16)),
        in_specs=[pl.BlockSpec(memory_space=pltpu.SMEM)] + [place] * (len(flat) + len(after)),
        out_specs=pl.BlockSpec(memory_space=pltpu.VMEM),
        scratch_shapes=[pltpu.SemaphoreType.DMA((len(flat),))],
        compiler_params=pltpu.CompilerParams(vmem_limit_bytes=4 * 2**20),
        cost_estimate=pl.CostEstimate(flops=0, bytes_accessed=2 * 8 * n * n * 2, transcendentals=0),
    )(scalars, *[leave_out(x) if far else x for x in flat], *after)


def tied(value, after=()):
    place = pl.BlockSpec(memory_space=pl.ANY)
    return pl.pallas_call(
        lambda *refs: None,
        out_shape=jax.ShapeDtypeStruct(value.shape, value.dtype),
        in_specs=[place] * (1 + len(after)),
        out_specs=place,
        input_output_aliases={0: 0},
        cost_estimate=pl.CostEstimate(flops=0, bytes_accessed=0, transcendentals=0),
    )(value, *after)


def to_block(total, more, out):
    out[0][...] = total[...].astype(bf16)


def moments(total, more, out):
    n = total.shape[0]
    for k in [slice(i, i + n // 5) for i in range(0, n, n // 5)]:
        rotated = total[:, k]
        first = beta_value * more[0][:, k] + (1.0 - beta_value) * rotated
        second = beta_value * more[1][:, k] + (1.0 - beta_value) * rotated * rotated
        out[0][:, k] = first
        out[1][:, k] = second
        quotient = first / bias_fix / (jnp.sqrt(second / bias_fix) + eps_value)
        out[2][k, :] = quotient.astype(bf16).T


def turned(total, more, out):
    out[0][...] = total[...].astype(bf16).T


def placed_bases(mat, left, right):
    n = left.shape[0]
    block = jax.ShapeDtypeStruct((n, n), bf16)

    def body(s, left, right, one, two, x, y, sems):
        copies = [pltpu.make_async_copy(left, x, sems.at[0]), pltpu.make_async_copy(right, y, sems.at[1])]
        for copy in copies:
            copy.start()
        for copy in copies:
            copy.wait()

        @pl.when(s[0] == 0)
        def _():
            one[...] = x[...].T
            two[...] = y[...]

        @pl.when(s[0] == 1)
        def _():
            one[...] = y[...]
            two[...] = x[...].T

    place, vmem = pl.BlockSpec(memory_space=pl.ANY), pl.BlockSpec(memory_space=pltpu.VMEM)
    return pl.pallas_call(
        body,
        out_shape=[kept_array(block)] * 2,
        in_specs=[pl.BlockSpec(memory_space=pltpu.SMEM), place, place],
        out_specs=[vmem] * 2,
        scratch_shapes=[pltpu.VMEM((n, n), bf16), pltpu.VMEM((n, n), bf16), pltpu.SemaphoreType.DMA((2,))],
        compiler_params=pltpu.CompilerParams(vmem_limit_bytes=8 * 2**20),
        cost_estimate=pl.CostEstimate(flops=0, bytes_accessed=4 * n * n * 2, transcendentals=0),
    )(mat, leave_out(left), leave_out(right))


def shards(gradient, left_basis, right_basis, first_moment, second_moment):
    grad, left, right = gradient[0], left_basis[0], right_basis[0]
    mat = lax.axis_index("mat").astype(jnp.int32)
    a, b = ("col", "row"), ("row", "col")

    def scalars(gathers, axes):
        return jnp.stack([mat if gathers else 1 - mat] + [member(axes, p) for p in PLACES])

    slot2, slot4, slot5, slot6 = scalars(0, b), scalars(1, a), scalars(0, a), scalars(1, b)
    n = grad.shape[0]
    block, whole = jax.ShapeDtypeStruct((n, n), bf16), jax.ShapeDtypeStruct((n, n), f32)
    one, two = placed_bases(mat[None], left, right)

    across, up, down = send(one, a, 0), send(one, a, 1), send(one, a, -1)
    upb, downb = send(two, b, 1), send(two, b, -1)
    relay = tied(across, (up, down, upb, downb))
    up1, down1, up2 = send(relay, a, 1), send(relay, a, -1), send(up, a, 1)
    two = tied(two, (relay,))
    acrossb = send(two, b, 0)
    down2 = send(down1, a, -1)
    gathered_a = (one, down, up2, up, relay, down1, down2, up1)
    weights_a = stacked(slot5, gathered_a)

    first = call(write_first, [block] * 2, slot2, weights_a, grad, flops=4 * n**3)
    upb1, downb1 = send(acrossb, b, 1), send(acrossb, b, -1)
    upb2 = send(upb, b, 1)
    overb = send(upb2, b, 0)
    weights_b = stacked(slot2, (two, downb, upb2, upb, acrossb, downb1, overb, upb1))
    middle, *first = both(
        b, 0, slot2, weights_a, grad, first, to_block, (), [block], 0, (slot4, weights_b), (upb2,),
        (downb1, overb),
    )
    new_first, new_second, normalized, *first = both(
        a, 1, slot4, weights_b, middle, first, moments, (first_moment[0], second_moment[0]), [whole, whole, block],
        2, (slot5, weights_b),
    )
    weights_a = stacked(slot5, gathered_a, (normalized,), True)
    middle, *first = both(
        a, 0, slot5, weights_b, normalized, first, to_block, (), [block], 0, (slot6, weights_a), (), (weights_a,)
    )
    (update,) = both(b, 1, slot6, weights_a, middle, first, turned, (), [block], 1)
    return update[None], new_first[None], new_second[None]


def solution(mesh):
    placed = (
        P("mat", "row", "col"),
        P("mat", "col", "row"),
        P("mat", "col", "row"),
        P("mat", "row", "col"),
        P("mat", "row", "col"),
    )
    return jax.shard_map(
        shards,
        mesh=mesh,
        in_specs=placed,
        out_specs=(P("mat", "row", "col"), P("mat", "row", "col"), P("mat", "row", "col")),
        check_vma=False,
    )
```

```python
import functools
import jax
import jax.numpy as jnp
from jax import lax
from jax.experimental import pallas as pl
from jax.experimental.pallas import tpu as pltpu
from jax.sharding import PartitionSpec as P

beta_value = 0.95
bias_fix = 1.0 - 0.95**10
eps_value = 1e-08

AXES = ("row", "col", "mat")
RING, PAIR = 4, 2
S0, S1, S2, S3 = (0, 0), (1, 0), (2, 0), (3, 0)
O0, O1, O2, O3 = (0, 1), (1, 1), (2, 1), (3, 1)
PLACES = (S0, S1, S2, S3, O0, O1, O2, O3)
f32, bf16 = jnp.float32, jnp.bfloat16


def split_index(axis, index):
    return (index // PAIR, index % PAIR) if axis == "row" else (index % RING, index // RING)


def join_index(axis, ring, pair):
    return ring * PAIR + pair if axis == "row" else pair * RING + ring


def pairs(axes, move):
    out = []
    for row in range(8):
        for col in range(8):
            for mat in range(2):
                axis = axes[mat]
                if axis is None:
                    continue
                ring, pair = split_index(axis, row if axis == "row" else col)
                ring, pair = ((ring + move) % RING, pair) if move else (ring, 1 - pair)
                there = join_index(axis, ring, pair)
                to = (there, col) if axis == "row" else (row, there)
                out.append(((row * 8 + col) * 2 + mat, (to[0] * 8 + to[1]) * 2 + mat))
    return out


def send(value, axes, move):
    return lax.ppermute(value, AXES, pairs(axes, move))


def member(axes, place):
    found = []
    for axis in axes:
        ring, pair = split_index(axis, lax.axis_index(axis))
        found.append(join_index(axis, (ring + place[0]) % RING, (pair + place[1]) % PAIR))
    return jnp.where(lax.axis_index("mat") == 0, found[0], found[1]).astype(jnp.int32)


def chunks(n):
    return [slice(i, min(i + 256, n)) for i in range(0, n, 256)]


def stay(x):
    return pltpu.with_memory_space_constraint(x, pltpu.VMEM)


def leave_out(x):
    return pltpu.with_memory_space_constraint(x, pltpu.HBM)


def kept_array(x):
    return pltpu.VMEM(x.shape, x.dtype)


def call(body, outs, *args, flops=0, scratch=(), after=(), leave=0, loose=0):
    vmem, place = pl.BlockSpec(memory_space=pltpu.VMEM), pl.BlockSpec(memory_space=pl.ANY)
    inputs = len(args)
    held = sum(x.size * x.dtype.itemsize for x in (*args[1:], *outs[:leave], *scratch) if x.ndim == 2)

    def whole(*refs):
        body(*refs[:inputs], *refs[inputs + len(after) :])

    return pl.pallas_call(
        whole,
        out_shape=[x if i < leave else kept_array(x) for i, x in enumerate(outs)],
        in_specs=[pl.BlockSpec(memory_space=pltpu.SMEM)] + [vmem] * (inputs - 1) + [place] * len(after),
        out_specs=[vmem] * len(outs),
        scratch_shapes=[pltpu.VMEM(x.shape, x.dtype) for x in scratch],
        compiler_params=pltpu.CompilerParams(vmem_limit_bytes=held + 4 * 2**20),
        cost_estimate=pl.CostEstimate(flops=flops, bytes_accessed=0, transcendentals=0),
    )(args[0], *[x if i < loose else stay(x) for i, x in enumerate(args[1:])], *after)


def block_of(scalars, place):
    return scalars[1 + PLACES.index(place)]


def write_term(own, w, index, out):
    for n in chunks(out.shape[1]):
        out[:, n] = jnp.dot(own[...], w[index, :, n], preferred_element_type=f32).astype(bf16)


def weighed(s, w, pairs, n):
    parts = [jnp.dot(w[block_of(s, p)], x[:, n], preferred_element_type=f32) for p, x in pairs]
    while len(parts) > 1:
        parts = [a + b for a, b in zip(parts[0::2], parts[1::2], strict=True)]
    return parts[0]


def write_first(s, w, own, u, d):
    @pl.when(s[0] == 1)
    def _():
        u[...] = own[...]
        d[...] = own[...]

    @pl.when(s[0] == 0)
    def _():
        write_term(own, w, block_of(s, O2), u)
        write_term(own, w, block_of(s, S2), d)


def both(axes, gathers, scalars, weights, own, first, finish, extra, outs, leave=0, following=None, early=(), late=()):
    one = tuple(a if m == gathers else None for m, a in enumerate(axes))
    other = tuple(a if m != gathers else None for m, a in enumerate(axes))
    n = own.shape[1]
    block = jax.ShapeDtypeStruct(own.shape, bf16)
    acc = jax.ShapeDtypeStruct((n, n), f32)
    cost = 2 * n**3
    u, d = first
    across, up, down = send(own, one, 0), send(u, axes, 1), send(d, axes, -1)

    kept = (O1, O3, O0, S1, S3, S0)

    def terms_body(s, w, a, *out):
        @pl.when(s[0] == 0)
        def _():
            for place, o in zip(kept, out, strict=True):
                write_term(a, w, block_of(s, place), o)

    term = dict(zip(kept, call(terms_body, [block] * 6, scalars, weights, own, flops=6 * cost), strict=True))

    def step1_body(s, c, u, p1, p3, q1, ou, od, ou2):
        @pl.when(s[0] == 1)
        def _():
            ou[...] = c[...]
            od[...] = c[...]
            ou2[...] = u[...]

        @pl.when(s[0] == 0)
        def _():
            ou[...] = (p1[...].astype(f32) + u[...].astype(f32)).astype(bf16)
            od[...] = p3[...]
            ou2[...] = q1[...]

    u, d, third = call(
        step1_body, [block] * 3, scalars, across, up, term[O1], term[O3], term[S1], after=early
    )
    up1, down1 = send(u, axes, 1), send(d, axes, -1)

    def weigh1_body(s, w, o, u, d, c, out):
        @pl.when(s[0] == 1)
        def _():
            for k in chunks(n):
                out[:, k] = weighed(s, w, ((S0, o), (S3, u), (S1, d), (O0, c)), k)

    total = call(weigh1_body, [acc], scalars, weights, own, up, down, across, flops=4 * cost)[0]

    def step2_body(s, d, u1, d1, p0, q3, oo, od):
        @pl.when(s[0] == 1)
        def _():
            od[...] = d1[...]

        @pl.when(s[0] == 0)
        def _():
            oo[...] = (p0[...].astype(f32) + u1[...].astype(f32) + d1[...].astype(f32)).astype(bf16)
            od[...] = (q3[...].astype(f32) + d[...].astype(f32)).astype(bf16)

    o, d = call(
        step2_body, [block] * 2, scalars, down, up1, down1, term[O0], term[S3], after=(total, *late)
    )
    over, up2, down2 = send(o, other, 0), send(third, axes, 1), send(d, axes, -1)

    def weigh2_body(s, w, t, u, d, out):
        @pl.when(s[0] == 1)
        def _():
            for k in chunks(n):
                out[:, k] = t[:, k] + weighed(s, w, ((O3, u), (O1, d)), k)

    total = call(weigh2_body, [acc], scalars, weights, total, up1, down1, flops=2 * cost, after=(over,))[0]
    ahead = [] if following is None else following
    opened = [block] * len(ahead)

    def last_body(s, w, t, u, d, p, c, *refs):
        then, refs = refs[: len(ahead)], refs[len(ahead) :]
        more, refs = refs[: len(extra)], refs[len(extra) :]
        out, begin, scratch = refs[: len(outs)], refs[len(outs) : -1], refs[-1]

        @pl.when(s[0] == 1)
        def _():
            for k in chunks(n):
                scratch[:, k] = t[:, k] + weighed(s, w, ((S2, u), (O2, d)), k)

        @pl.when(s[0] == 0)
        def _():
            parts = [x[...].astype(f32) for x in (p, c, u, d)]
            scratch[...] = (parts[0] + parts[1]) + (parts[2] + parts[3])

        finish(scratch, more, out)
        if ahead:
            write_first(*then, out[-1], *begin)

    return call(
        last_body, [*outs, *opened], scalars, weights, total, up2, down2, term[S0], over, *ahead, *extra,
        flops=2 * cost, scratch=[acc], leave=leave,
    )


def stacked(scalars, blocks, after=(), far=False):
    flat = [x for block in blocks for x in (block if isinstance(block, tuple) else (block,))]
    n = flat[0].shape[1]

    def body(s, *refs):
        out, sems, copies, at = refs[-2], refs[-1], [], 0
        for place, block in zip(PLACES, blocks, strict=True):
            row = 0
            for x in block if isinstance(block, tuple) else (block,):
                target = out.at[block_of(s, place), pl.ds(row, x.shape[0])]
                copies.append(pltpu.make_async_copy(refs[at], target, sems.at[at]))
                row += x.shape[0]
                at += 1
        for copy in copies:
            copy.start()
        for copy in copies:
            copy.wait()

    place = pl.BlockSpec(memory_space=pl.ANY)
    return pl.pallas_call(
        lambda s, *refs: body(s, *refs[: len(flat)], *refs[len(flat) + len(after) :]),
        out_shape=kept_array(jax.ShapeDtypeStruct((8, n, n), bf16)),
        in_specs=[pl.BlockSpec(memory_space=pltpu.SMEM)] + [place] * (len(flat) + len(after)),
        out_specs=pl.BlockSpec(memory_space=pltpu.VMEM),
        scratch_shapes=[pltpu.SemaphoreType.DMA((len(flat),))],
        compiler_params=pltpu.CompilerParams(vmem_limit_bytes=4 * 2**20),
        cost_estimate=pl.CostEstimate(flops=0, bytes_accessed=2 * 8 * n * n * 2, transcendentals=0),
    )(scalars, *[leave_out(x) if far else x for x in flat], *after)


def tied(value, after=()):
    place = pl.BlockSpec(memory_space=pl.ANY)
    return pl.pallas_call(
        lambda *refs: None,
        out_shape=jax.ShapeDtypeStruct(value.shape, value.dtype),
        in_specs=[place] * (1 + len(after)),
        out_specs=place,
        input_output_aliases={0: 0},
        cost_estimate=pl.CostEstimate(flops=0, bytes_accessed=0, transcendentals=0),
    )(value, *after)


def to_block(total, more, out):
    out[0][...] = total[...].astype(bf16)


def moments(total, more, out):
    n = total.shape[0]
    for k in [slice(i, i + n // 5) for i in range(0, n, n // 5)]:
        rotated = total[:, k]
        first = beta_value * more[0][:, k] + (1.0 - beta_value) * rotated
        second = beta_value * more[1][:, k] + (1.0 - beta_value) * rotated * rotated
        out[0][:, k] = first
        out[1][:, k] = second
        quotient = first / bias_fix / (jnp.sqrt(second / bias_fix) + eps_value)
        out[2][k, :] = quotient.astype(bf16).T


def turned(total, more, out):
    out[0][...] = total[...].astype(bf16).T


def placed_bases(mat, left, right):
    n = left.shape[0]
    block = jax.ShapeDtypeStruct((n, n), bf16)

    def body(s, left, right, one, two, x, y, sems):
        copies = [pltpu.make_async_copy(left, x, sems.at[0]), pltpu.make_async_copy(right, y, sems.at[1])]
        for copy in copies:
            copy.start()
        for copy in copies:
            copy.wait()

        @pl.when(s[0] == 0)
        def _():
            one[...] = x[...].T
            two[...] = y[...]

        @pl.when(s[0] == 1)
        def _():
            one[...] = y[...]
            two[...] = x[...].T

    place, vmem = pl.BlockSpec(memory_space=pl.ANY), pl.BlockSpec(memory_space=pltpu.VMEM)
    return pl.pallas_call(
        body,
        out_shape=[kept_array(block)] * 2,
        in_specs=[pl.BlockSpec(memory_space=pltpu.SMEM), place, place],
        out_specs=[vmem] * 2,
        scratch_shapes=[pltpu.VMEM((n, n), bf16), pltpu.VMEM((n, n), bf16), pltpu.SemaphoreType.DMA((2,))],
        compiler_params=pltpu.CompilerParams(vmem_limit_bytes=8 * 2**20),
        cost_estimate=pl.CostEstimate(flops=0, bytes_accessed=4 * n * n * 2, transcendentals=0),
    )(mat, leave_out(left), leave_out(right))


def shards(gradient, left_basis, right_basis, first_moment, second_moment):
    grad, left, right = gradient[0], left_basis[0], right_basis[0]
    mat = lax.axis_index("mat").astype(jnp.int32)
    a, b = ("col", "row"), ("row", "col")

    def scalars(gathers, axes):
        return jnp.stack([mat if gathers else 1 - mat] + [member(axes, p) for p in PLACES])

    slot2, slot4, slot5, slot6 = scalars(0, b), scalars(1, a), scalars(0, a), scalars(1, b)
    n = grad.shape[0]
    block, whole = jax.ShapeDtypeStruct((n, n), bf16), jax.ShapeDtypeStruct((n, n), f32)
    one, two = placed_bases(mat[None], left, right)

    across, up, down = send(one, a, 0), send(one, a, 1), send(one, a, -1)
    upb, downb = send(two, b, 1), send(two, b, -1)
    relay = tied(across, (up, down, upb, downb))
    up1, down1, up2 = send(relay, a, 1), send(relay, a, -1), send(up, a, 1)
    two = tied(two, (relay,))
    acrossb = send(two, b, 0)
    down2 = send(down1, a, -1)
    gathered_a = (one, down, up2, up, relay, down1, down2, up1)
    weights_a = stacked(slot5, gathered_a)

    first = call(write_first, [block] * 2, slot2, weights_a, grad, flops=4 * n**3)
    upb1, downb1 = send(acrossb, b, 1), send(acrossb, b, -1)
    upb2 = send(upb, b, 1)
    downb2 = send(downb1, b, -1)
    weights_b = stacked(slot2, (two, downb, upb2, upb, acrossb, downb1, downb2, upb1))
    middle, *first = both(
        b, 0, slot2, weights_a, grad, first, to_block, (), [block], 0, (slot4, weights_b), (),
        (upb2, downb1),
    )
    new_first, new_second, normalized, *first = both(
        a, 1, slot4, weights_b, middle, first, moments, (first_moment[0], second_moment[0]), [whole, whole, block],
        2, (slot5, weights_b),
    )
    weights_a = stacked(slot5, gathered_a, (normalized,), True)
    middle, *first = both(
        a, 0, slot5, weights_b, normalized, first, to_block, (), [block], 0, (slot6, weights_a), (), (weights_a,)
    )
    (update,) = both(b, 1, slot6, weights_a, middle, first, turned, (), [block], 1)
    return update[None], new_first[None], new_second[None]


def solution(mesh):
    placed = (
        P("mat", "row", "col"),
        P("mat", "col", "row"),
        P("mat", "col", "row"),
        P("mat", "row", "col"),
        P("mat", "row", "col"),
    )
    return jax.shard_map(
        shards,
        mesh=mesh,
        in_specs=placed,
        out_specs=(P("mat", "row", "col"), P("mat", "row", "col"), P("mat", "row", "col")),
        check_vma=False,
    )
```
